128 devices in a mesh: shot: 8 (over x_hi, y), rcv: 16 (over x_lo, z, core).
Axes of the slice: x: 4 (x_hi: 2, x_lo: 2; x = x_hi * 2 + x_lo), y: 4, z: 4, core: 2. Of those that a mesh axis runs over, the one named last changes fastest.
Arguments:
- surface_data: bfloat16 [4, 2, 512, 8192], P(None, None, 'rcv', 'shot'), may hold values from -6 to 6
- source_traces: bfloat16 [4, 2, 512, 8192], P(None, None, 'shot', 'rcv'), may hold values from -0.21875 to 0.21875
- block_ids: int32 [12], replicated, may hold values from 0 to 15
Outputs:
- multiples: bfloat16 [4, 2, 8192, 8192], P(None, None, 'shot', 'rcv')
The draws below stay inside these ranges and needn't reach their ends.
All inputs are finite; a program needn't handle non-finite values.
Results may differ from the reference program's by a relative error of at most 0.001.
Values may be sent and summed in bfloat16 or wider, within the bound.
No kernel may reach another device: no remote copies, remote signals or barrier semaphores. Data moves between devices by JAX's collectives and lax.ppermute only.
A program may use at most 128 MiB of HBM per device.

```python
import jax
import jax.numpy as jnp
from jax import lax

F = 4
BLK = 32
STEPS = 12
SHOTS = 8192
RCVS = 8192
KPTS = 512
N_RCV = 16


def with_ends(result, stream_key, least, largest):
    longest = result.shape.index(max(result.shape))
    spots = []
    for shift in (0, 1):
        where = [jax.random.randint(jax.random.fold_in(stream_key, axis), (), 0, length) for axis, length in enumerate(result.shape)]
        where[longest] = (where[longest] + shift) % result.shape[longest]
        spots.append(tuple(where))
    return result.at[spots[0]].set(least).at[spots[1]].set(largest)


def shard_levels(key, dims, cuts, smallest, largest):
    factor_of, own = 1.0, jax.random.fold_in(key, 6)
    for position, shards_of in cuts:
        heights = jnp.exp(jax.random.uniform(jax.random.fold_in(own, position), (shards_of,), jnp.float32, smallest / len(cuts), largest / len(cuts)))
        factor_of = factor_of * jnp.repeat(heights, dims[position] // shards_of).reshape([-1 if axis == position else 1 for axis in range(len(dims))])
    return factor_of


def centred(stream_key, extent, deviation, reach, split=(), held_as=jnp.bfloat16):
    result = deviation * jax.random.normal(stream_key, extent, jnp.float32)
    if split:
        result = result * shard_levels(stream_key, extent, split, -0.22, 0.18)
    return jnp.clip(result, -reach, reach).astype(held_as)


def setup_inputs(seed: int = 0) -> dict:
    streams_of = jax.random.split(jax.random.key(seed), 4)
    surface_data = centred(streams_of[0], (F, 2, KPTS, SHOTS), 1.0, 6.0, ((2, 16), (3, 8)))
    source_traces = centred(streams_of[1], (F, 2, KPTS, RCVS), (2 * STEPS * BLK) ** -0.5, 0.21875, ((2, 8), (3, 16)))
    block_ids = with_ends(jax.random.randint(streams_of[2], (STEPS,), 0, N_RCV), jax.random.fold_in(streams_of[2], 1), 0, N_RCV - 1).astype(jnp.int32)
    return {"surface_data": surface_data, "source_traces": source_traces, "block_ids": block_ids}


def reference(surface_data, source_traces, block_ids):
    points = (block_ids[:, None] * BLK + jnp.arange(BLK, dtype=jnp.int32)[None, :]).reshape(-1).astype(jnp.int32)

    def one_freq(f):
        left = jnp.take(surface_data[f], points, axis=1)
        right = jnp.take(source_traces[f], points, axis=1)
        real_part = jnp.dot(left[0].T, right[0], preferred_element_type=jnp.float32) - jnp.dot(left[1].T, right[1], preferred_element_type=jnp.float32)
        imag_part = jnp.dot(left[0].T, right[1], preferred_element_type=jnp.float32) + jnp.dot(left[1].T, right[0], preferred_element_type=jnp.float32)
        return jnp.stack([real_part, imag_part]).astype(jnp.bfloat16)

    return lax.map(one_freq, jnp.arange(F, dtype=jnp.int32))
```

```python
import jax
import jax.numpy as jnp
from jax import lax
from jax.experimental import pallas as pl
from jax.experimental.pallas import tpu as pltpu
from jax.sharding import PartitionSpec as P

BLK = 32
STEPS = 12
ROWS = 256
AXES = ("shot", "rcv")
X, Y, Z, CORES = 4, 4, 4, 2


def moved(value, dx=0, dy=0, dz=0, flip_x=False, flip_core=False):
    def index(x, y, z, core):
        x_hi, x_lo = divmod(x, 2)
        return (((x_hi * Y + y) * 2 + x_lo) * Z + z) * CORES + core

    pairs = []
    for x in range(X):
        for y in range(Y):
            for z in range(Z):
                for core in range(CORES):
                    way = 1 - 2 * core
                    to_x = x ^ 1 if flip_x else (x + way * dx) % X
                    to_core = core ^ 1 if flip_core else core
                    target = index(to_x, (y + way * dy) % Y, (z + way * dz) % Z, to_core)
                    pairs.append((index(x, y, z, core), target))
    return lax.ppermute(value, AXES, pairs)


def choose(refs, which, act):
    if len(refs) == 1:
        act(refs[0])
        return
    half = len(refs) // 2

    @pl.when(which < half)
    def _():
        choose(refs[:half], which, act)

    @pl.when(which >= half)
    def _():
        choose(refs[half:], which - half, act)


def multiply_kernel(a_where, b_where, b_row, *refs):
    a_refs, b_refs = refs[:16], refs[16:24]
    out, a_buf, b_buf, lhs, rhs, a_sem, b_sem = refs[24:]
    freqs = a_buf.shape[1]
    f = pl.program_id(0)
    rcvs = b_buf.shape[4]

    def fetch(first_freq, count, slot):
        these = pl.ds(first_freq, count)
        for step in range(STEPS):

            def from_surface(ref):
                pltpu.make_async_copy(
                    ref.at[these], a_buf.at[step, these], a_sem.at[slot]
                ).start()

            choose(a_refs, a_where[step], from_surface)

            def from_traces(ref):
                first = pl.multiple_of(b_row[step], BLK)
                pltpu.make_async_copy(
                    ref.at[these, :, pl.ds(first, BLK)], b_buf.at[step, these], b_sem.at[slot]
                ).start()

            choose(b_refs, b_where[step], from_traces)

    def arrive(first_freq, count, slot):
        these = pl.ds(first_freq, count)
        for buf, sem in ((a_buf, a_sem), (b_buf, b_sem)):
            part = buf.at[:, these]
            pltpu.make_async_copy(part, part, sem.at[slot]).wait()

    @pl.when(f == 0)
    def _():
        fetch(0, 1, 0)
        fetch(1, freqs - 1, 1)
        arrive(0, 1, 0)

    @pl.when(f == 1)
    def _():
        arrive(1, freqs - 1, 1)

    for step in range(STEPS):
        real = b_buf[step, f, 0]
        imag = b_buf[step, f, 1]
        rhs[0, step, 0] = real
        rhs[0, step, 1] = -imag
        rhs[1, step, 0] = imag
        rhs[1, step, 1] = real

    depth = STEPS * 2 * BLK
    for first in range(0, lhs.shape[0], ROWS):
        block = a_buf[:, f, :, :, first : first + ROWS].reshape(depth, ROWS)
        lhs[first : first + ROWS, :] = block.T

    for part in range(2):
        out[0, part] = jnp.dot(
            lhs[...], rhs[part].reshape(depth, rcvs), preferred_element_type=jnp.float32
        ).astype(out.dtype)


def multiply(a_parts, b_parts, a_where, b_where, b_row):
    freqs, _, _, shots = a_parts[0].shape
    rcvs = b_parts[0].shape[3]
    depth = STEPS * 2 * BLK
    return pl.pallas_call(
        multiply_kernel,
        out_shape=jax.ShapeDtypeStruct((freqs, 2, shots, rcvs), jnp.bfloat16),
        grid_spec=pltpu.PrefetchScalarGridSpec(
            num_scalar_prefetch=3,
            grid=(freqs,),
            in_specs=[pl.BlockSpec(memory_space=pl.ANY)] * (len(a_parts) + len(b_parts)),
            out_specs=pl.BlockSpec((1, 2, shots, rcvs), lambda f, *_: (f, 0, 0, 0)),
            scratch_shapes=[
                pltpu.VMEM((STEPS, freqs, 2, BLK, shots), jnp.bfloat16),
                pltpu.VMEM((STEPS, freqs, 2, BLK, rcvs), jnp.bfloat16),
                pltpu.VMEM((shots, depth), jnp.bfloat16),
                pltpu.VMEM((2, STEPS, 2, BLK, rcvs), jnp.bfloat16),
                pltpu.SemaphoreType.DMA((2,)),
                pltpu.SemaphoreType.DMA((2,)),
            ],
        ),
        compiler_params=pltpu.CompilerParams(vmem_limit_bytes=56 * 1024 * 1024),
        cost_estimate=pl.CostEstimate(
            flops=2 * freqs * shots * 2 * rcvs * depth,
            bytes_accessed=20 * 1024 * 1024,
            transcendentals=0,
        ),
    )(a_where, b_where, b_row, *a_parts, *b_parts)


def places(block_ids):
    shot, rcv = lax.axis_index("shot"), lax.axis_index("rcv")
    core, z, x_lo = rcv % CORES, rcv // CORES % Z, rcv // (CORES * Z)
    of_core, of_z, of_x = block_ids % CORES, block_ids // CORES % Z, block_ids // (CORES * Z)
    distance = jnp.where(of_core == 0, z - of_z, of_z - z) % Z
    a_where = ((of_core != core) * 2 + (of_x != x_lo)) * Z + distance
    owner = block_ids // 2
    y, of_y = shot % Y, owner % Y
    distance = jnp.where(core == 0, y - of_y, of_y - y) % Y
    b_where = (shot // Y != owner // Y) * Y + distance
    return a_where.astype(jnp.int32), b_where.astype(jnp.int32), block_ids % 2 * BLK


def after(value, *earlier):
    return lax.optimization_barrier((value, *earlier))[0]


def per_device(surface_data, source_traces, block_ids):
    a, b = surface_data, source_traces

    def send(name, value, **way):
        with jax.named_scope(name):
            return moved(value, **way)

    def swap(name, value):
        return send(name, value, flip_core=True)

    b_hop = send("b_hop", b, dx=1)
    b_1 = send("b_1", b, dy=1)
    a_1 = send("a_1", a, dz=1)
    b_x = send("b_x", b_hop, dx=1)
    a_x = send("a_x", after(a, b_x), flip_x=True)
    a_2 = send("a_2", a_1, dz=1)
    a_3 = send("a_3", after(a, a_2), dz=-1)
    b_x1 = send("b_x1", b_x, dy=1)
    b_x2 = send("b_x2", b_x1, dy=1)
    a_x1 = send("a_x1", a_x, dz=1)
    a_x3 = send("a_x3", after(a_x, a_2), dz=-1)
    a_x2 = send("a_x2", a_2, flip_x=True)
    other = swap("other", a)
    b_3 = send("b_3", after(b, other), dy=-1)
    b_2 = send("b_2", after(b_1, b_3, a_2), dy=1)
    b_x3 = send("b_x3", after(b_x, b_2), dy=-1)
    other_1 = swap("other_1", after(a_1, a_2))
    other_2 = swap("other_2", after(a_2, a_3))
    other_3 = swap("other_3", after(a_3, b_2))
    other_x = swap("other_x", after(a_x, a_x3, b_x2, b_2))
    other_x1 = swap("other_x1", after(a_x1, b_1))
    other_x2 = swap("other_x2", after(a_x2, b_1))
    other_x3 = swap("other_x3", after(a_x3, other_3))

    a_parts = [a, a_1, a_2, a_3, a_x, a_x1, a_x2, a_x3]
    a_parts += [other, other_1, other_2, other_3, other_x, other_x1, other_x2, other_x3]
    b_parts = [b, b_1, b_2, b_3, b_x, b_x1, b_x2, b_x3]
    return multiply(a_parts, b_parts, *places(block_ids))


def solution(mesh):
    in_specs = (P(None, None, "rcv", "shot"), P(None, None, "shot", "rcv"), P())
    out_specs = P(None, None, "shot", "rcv")
    return jax.shard_map(
        per_device, mesh=mesh, in_specs=in_specs, out_specs=out_specs, check_vma=False
    )
```

```python
import jax
import jax.numpy as jnp
from jax import lax
from jax.experimental import pallas as pl
from jax.experimental.pallas import tpu as pltpu
from jax.sharding import PartitionSpec as P

BLK = 32
STEPS = 12
ROWS = 256
AXES = ("shot", "rcv")
X, Y, Z, CORES = 4, 4, 4, 2


def moved(value, dx=0, dy=0, dz=0, flip_x=False, flip_core=False):
    def index(x, y, z, core):
        x_hi, x_lo = divmod(x, 2)
        return (((x_hi * Y + y) * 2 + x_lo) * Z + z) * CORES + core

    pairs = []
    for x in range(X):
        for y in range(Y):
            for z in range(Z):
                for core in range(CORES):
                    way = 1 - 2 * core
                    to_x = x ^ 1 if flip_x else (x + way * dx) % X
                    to_core = core ^ 1 if flip_core else core
                    target = index(to_x, (y + way * dy) % Y, (z + way * dz) % Z, to_core)
                    pairs.append((index(x, y, z, core), target))
    return lax.ppermute(value, AXES, pairs)


def choose(refs, which, act):
    if len(refs) == 1:
        act(refs[0])
        return
    half = len(refs) // 2

    @pl.when(which < half)
    def _():
        choose(refs[:half], which, act)

    @pl.when(which >= half)
    def _():
        choose(refs[half:], which - half, act)


def multiply_kernel(a_where, b_where, b_row, *refs):
    a_refs, b_refs = refs[:16], refs[16:24]
    out, a_buf, b_buf, lhs, rhs, a_sem, b_sem = refs[24:]
    freqs = a_buf.shape[1]
    f = pl.program_id(0)
    rcvs = b_buf.shape[4]

    def fetch(first_freq, count, slot):
        these = pl.ds(first_freq, count)
        for step in range(STEPS):

            def from_surface(ref):
                pltpu.make_async_copy(
                    ref.at[these], a_buf.at[step, these], a_sem.at[slot]
                ).start()

            choose(a_refs, a_where[step], from_surface)

            def from_traces(ref):
                first = pl.multiple_of(b_row[step], BLK)
                pltpu.make_async_copy(
                    ref.at[these, :, pl.ds(first, BLK)], b_buf.at[step, these], b_sem.at[slot]
                ).start()

            choose(b_refs, b_where[step], from_traces)

    def arrive(first_freq, count, slot):
        these = pl.ds(first_freq, count)
        for buf, sem in ((a_buf, a_sem), (b_buf, b_sem)):
            part = buf.at[:, these]
            pltpu.make_async_copy(part, part, sem.at[slot]).wait()

    @pl.when(f == 0)
    def _():
        fetch(0, 1, 0)
        fetch(1, freqs - 1, 1)
        arrive(0, 1, 0)

    @pl.when(f == 1)
    def _():
        arrive(1, freqs - 1, 1)

    for step in range(STEPS):
        real = b_buf[step, f, 0]
        imag = b_buf[step, f, 1]
        rhs[0, step, 0] = real
        rhs[0, step, 1] = -imag
        rhs[1, step, 0] = imag
        rhs[1, step, 1] = real

    depth = STEPS * 2 * BLK
    for first in range(0, lhs.shape[0], ROWS):
        block = a_buf[:, f, :, :, first : first + ROWS].reshape(depth, ROWS)
        lhs[first : first + ROWS, :] = block.T

    for part in range(2):
        out[0, part] = jnp.dot(
            lhs[...], rhs[part].reshape(depth, rcvs), preferred_element_type=jnp.float32
        ).astype(out.dtype)


def multiply(a_parts, b_parts, a_where, b_where, b_row):
    freqs, _, _, shots = a_parts[0].shape
    rcvs = b_parts[0].shape[3]
    depth = STEPS * 2 * BLK
    return pl.pallas_call(
        multiply_kernel,
        out_shape=jax.ShapeDtypeStruct((freqs, 2, shots, rcvs), jnp.bfloat16),
        grid_spec=pltpu.PrefetchScalarGridSpec(
            num_scalar_prefetch=3,
            grid=(freqs,),
            in_specs=[pl.BlockSpec(memory_space=pl.ANY)] * (len(a_parts) + len(b_parts)),
            out_specs=pl.BlockSpec((1, 2, shots, rcvs), lambda f, *_: (f, 0, 0, 0)),
            scratch_shapes=[
                pltpu.VMEM((STEPS, freqs, 2, BLK, shots), jnp.bfloat16),
                pltpu.VMEM((STEPS, freqs, 2, BLK, rcvs), jnp.bfloat16),
                pltpu.VMEM((shots, depth), jnp.bfloat16),
                pltpu.VMEM((2, STEPS, 2, BLK, rcvs), jnp.bfloat16),
                pltpu.SemaphoreType.DMA((2,)),
                pltpu.SemaphoreType.DMA((2,)),
            ],
        ),
        compiler_params=pltpu.CompilerParams(vmem_limit_bytes=56 * 1024 * 1024),
        cost_estimate=pl.CostEstimate(
            flops=2 * freqs * shots * 2 * rcvs * depth,
            bytes_accessed=20 * 1024 * 1024,
            transcendentals=0,
        ),
    )(a_where, b_where, b_row, *a_parts, *b_parts)


def places(block_ids):
    shot, rcv = lax.axis_index("shot"), lax.axis_index("rcv")
    core, z, x_lo = rcv % CORES, rcv // CORES % Z, rcv // (CORES * Z)
    of_core, of_z, of_x = block_ids % CORES, block_ids // CORES % Z, block_ids // (CORES * Z)
    distance = jnp.where(of_core == 0, z - of_z, of_z - z) % Z
    a_where = ((of_core != core) * 2 + (of_x != x_lo)) * Z + distance
    owner = block_ids // 2
    y, of_y = shot % Y, owner % Y
    distance = jnp.where(core == 0, y - of_y, of_y - y) % Y
    b_where = (shot // Y != owner // Y) * Y + distance
    return a_where.astype(jnp.int32), b_where.astype(jnp.int32), block_ids % 2 * BLK


def after(value, *earlier):
    return lax.optimization_barrier((value, *earlier))[0]


def per_device(surface_data, source_traces, block_ids):
    a, b = surface_data, source_traces

    def send(name, value, **way):
        with jax.named_scope(name):
            return moved(value, **way)

    def swap(name, value):
        return send(name, value, flip_core=True)

    b_hop = send("b_hop", b, dx=1)
    b_1 = send("b_1", b, dy=1)
    b_3 = send("b_3", b, dy=-1)
    a_1 = send("a_1", a, dz=1)
    b_x = send("b_x", b_hop, dx=1)
    b_2 = send("b_2", b_1, dy=1)
    a_2 = send("a_2", a_1, dz=1)
    b_x1 = send("b_x1", b_x, dy=1)
    b_x2 = send("b_x2", b_x1, dy=1)
    a_x2 = send("a_x2", after(a_2, b_2), flip_x=True)
    other = swap("other", a)
    a_x = send("a_x", after(a, other), flip_x=True)
    other_1 = swap("other_1", after(a_1, b_3))
    a_3 = send("a_3", after(a, other_1), dz=-1)
    b_x3 = send("b_x3", after(b_x, a_3), dy=-1)
    other_2 = swap("other_2", a_2)
    a_x3 = send("a_x3", after(a_x, other_2), dz=-1)
    other_3 = swap("other_3", a_3)
    other_x = swap("other_x", a_x)
    a_x1 = send("a_x1", after(a_x, other_x), dz=1)
    other_x1 = swap("other_x1", after(a_x1, a_x2))
    other_x2 = swap("other_x2", after(a_x2, b_1))
    other_x3 = swap("other_x3", a_x3)

    a_parts = [a, a_1, a_2, a_3, a_x, a_x1, a_x2, a_x3]
    a_parts += [other, other_1, other_2, other_3, other_x, other_x1, other_x2, other_x3]
    b_parts = [b, b_1, b_2, b_3, b_x, b_x1, b_x2, b_x3]
    return multiply(a_parts, b_parts, *places(block_ids))


def solution(mesh):
    in_specs = (P(None, None, "rcv", "shot"), P(None, None, "shot", "rcv"), P())
    out_specs = P(None, None, "shot", "rcv")
    return jax.shard_map(
        per_device, mesh=mesh, in_specs=in_specs, out_specs=out_specs, check_vma=False
    )
```

```python
import jax
import jax.numpy as jnp
from jax import lax
from jax.experimental import pallas as pl
from jax.experimental.pallas import tpu as pltpu
from jax.sharding import PartitionSpec as P

BLK = 32
STEPS = 12
ROWS = 256
AXES = ("shot", "rcv")
X, Y, Z, CORES = 4, 4, 4, 2


def moved(value, dx=0, dy=0, dz=0, flip_x=False, flip_core=False):
    def index(x, y, z, core):
        x_hi, x_lo = divmod(x, 2)
        return (((x_hi * Y + y) * 2 + x_lo) * Z + z) * CORES + core

    pairs = []
    for x in range(X):
        for y in range(Y):
            for z in range(Z):
                for core in range(CORES):
                    way = 1 - 2 * core
                    to_x = x ^ 1 if flip_x else (x + way * dx) % X
                    to_core = core ^ 1 if flip_core else core
                    target = index(to_x, (y + way * dy) % Y, (z + way * dz) % Z, to_core)
                    pairs.append((index(x, y, z, core), target))
    return lax.ppermute(value, AXES, pairs)


def choose(refs, which, act):
    if len(refs) == 1:
        act(refs[0])
        return
    half = len(refs) // 2

    @pl.when(which < half)
    def _():
        choose(refs[:half], which, act)

    @pl.when(which >= half)
    def _():
        choose(refs[half:], which - half, act)


def multiply_kernel(a_where, b_where, b_row, *refs):
    a_refs, b_refs = refs[:16], refs[16:24]
    out, a_buf, b_buf, lhs, rhs, a_sem, b_sem = refs[24:]
    freqs = a_buf.shape[1]
    f = pl.program_id(0)
    rcvs = b_buf.shape[4]

    def fetch(first_freq, count, slot):
        these = pl.ds(first_freq, count)
        for step in range(STEPS):

            def from_surface(ref):
                pltpu.make_async_copy(
                    ref.at[these], a_buf.at[step, these], a_sem.at[slot]
                ).start()

            choose(a_refs, a_where[step], from_surface)

            def from_traces(ref):
                first = pl.multiple_of(b_row[step], BLK)
                pltpu.make_async_copy(
                    ref.at[these, :, pl.ds(first, BLK)], b_buf.at[step, these], b_sem.at[slot]
                ).start()

            choose(b_refs, b_where[step], from_traces)

    def arrive(first_freq, count, slot):
        these = pl.ds(first_freq, count)
        for buf, sem in ((a_buf, a_sem), (b_buf, b_sem)):
            part = buf.at[:, these]
            pltpu.make_async_copy(part, part, sem.at[slot]).wait()

    @pl.when(f == 0)
    def _():
        fetch(0, 1, 0)
        fetch(1, freqs - 1, 1)
        arrive(0, 1, 0)

    @pl.when(f == 1)
    def _():
        arrive(1, freqs - 1, 1)

    for step in range(STEPS):
        real = b_buf[step, f, 0]
        imag = b_buf[step, f, 1]
        rhs[0, step, 0] = real
        rhs[0, step, 1] = -imag
        rhs[1, step, 0] = imag
        rhs[1, step, 1] = real

    depth = STEPS * 2 * BLK
    for first in range(0, lhs.shape[0], ROWS):
        block = a_buf[:, f, :, :, first : first + ROWS].reshape(depth, ROWS)
        lhs[first : first + ROWS, :] = block.T

    for part in range(2):
        out[0, part] = jnp.dot(
            lhs[...], rhs[part].reshape(depth, rcvs), preferred_element_type=jnp.float32
        ).astype(out.dtype)


def multiply(a_parts, b_parts, a_where, b_where, b_row):
    freqs, _, _, shots = a_parts[0].shape
    rcvs = b_parts[0].shape[3]
    depth = STEPS * 2 * BLK
    return pl.pallas_call(
        multiply_kernel,
        out_shape=jax.ShapeDtypeStruct((freqs, 2, shots, rcvs), jnp.bfloat16),
        grid_spec=pltpu.PrefetchScalarGridSpec(
            num_scalar_prefetch=3,
            grid=(freqs,),
            in_specs=[pl.BlockSpec(memory_space=pl.ANY)] * (len(a_parts) + len(b_parts)),
            out_specs=pl.BlockSpec((1, 2, shots, rcvs), lambda f, *_: (f, 0, 0, 0)),
            scratch_shapes=[
                pltpu.VMEM((STEPS, freqs, 2, BLK, shots), jnp.bfloat16),
                pltpu.VMEM((STEPS, freqs, 2, BLK, rcvs), jnp.bfloat16),
                pltpu.VMEM((shots, depth), jnp.bfloat16),
                pltpu.VMEM((2, STEPS, 2, BLK, rcvs), jnp.bfloat16),
                pltpu.SemaphoreType.DMA((2,)),
                pltpu.SemaphoreType.DMA((2,)),
            ],
        ),
        compiler_params=pltpu.CompilerParams(vmem_limit_bytes=56 * 1024 * 1024),
        cost_estimate=pl.CostEstimate(
            flops=2 * freqs * shots * 2 * rcvs * depth,
            bytes_accessed=20 * 1024 * 1024,
            transcendentals=0,
        ),
    )(a_where, b_where, b_row, *a_parts, *b_parts)


def places(block_ids):
    shot, rcv = lax.axis_index("shot"), lax.axis_index("rcv")
    core, z, x_lo = rcv % CORES, rcv // CORES % Z, rcv // (CORES * Z)
    of_core, of_z, of_x = block_ids % CORES, block_ids // CORES % Z, block_ids // (CORES * Z)
    distance = jnp.where(of_core == 0, z - of_z, of_z - z) % Z
    a_where = ((of_core != core) * 2 + (of_x != x_lo)) * Z + distance
    owner = block_ids // 2
    y, of_y = shot % Y, owner % Y
    distance = jnp.where(core == 0, y - of_y, of_y - y) % Y
    b_where = (shot // Y != owner // Y) * Y + distance
    return a_where.astype(jnp.int32), b_where.astype(jnp.int32), block_ids % 2 * BLK


def after(value, *earlier):
    return lax.optimization_barrier((value, *earlier))[0]


def per_device(surface_data, source_traces, block_ids):
    a, b = surface_data, source_traces

    def send(name, value, **way):
        with jax.named_scope(name):
            return moved(value, **way)

    def swap(name, value):
        return send(name, value, flip_core=True)

    a_1 = send("a_1", a, dz=1)
    b_x = send("b_x", b, dx=2)
    a_3 = send("a_3", a, dz=-1)
    b_3 = send("b_3", b, dy=-1)
    b_1 = send("b_1", b, dy=1)
    a_x = send("a_x", after(a, a_1), flip_x=True)
    b_x1 = send("b_x1", b_x, dy=1)
    other = swap("other", after(a, a_3))
    a_2 = send("a_2", after(a_1, b_3), dz=1)
    b_2 = send("b_2", b_1, dy=1)
    other_3 = swap("other_3", after(a_3, a_x))
    other_x = swap("other_x", after(a_x, b_x1))
    a_x1 = send("a_x1", after(a_x, other), dz=1)
    a_x2 = send("a_x2", a_2, flip_x=True)
    b_x3 = send("b_x3", after(b_x, b_2), dy=-1)
    a_x3 = send("a_x3", after(a_x, other_3), dz=-1)
    b_x2 = send("b_x2", after(b_x1, other_x), dy=1)
    other_x1 = swap("other_x1", a_x1)
    other_1 = swap("other_1", after(a_1, a_x2))
    other_2 = swap("other_2", after(a_2, b_x3))
    other_x3 = swap("other_x3", a_x3)
    other_x2 = swap("other_x2", after(a_x2, b_x2))

    a_parts = [a, a_1, a_2, a_3, a_x, a_x1, a_x2, a_x3]
    a_parts += [other, other_1, other_2, other_3, other_x, other_x1, other_x2, other_x3]
    b_parts = [b, b_1, b_2, b_3, b_x, b_x1, b_x2, b_x3]
    return multiply(a_parts, b_parts, *places(block_ids))


def solution(mesh):
    in_specs = (P(None, None, "rcv", "shot"), P(None, None, "shot", "rcv"), P())
    out_specs = P(None, None, "shot", "rcv")
    return jax.shard_map(
        per_device, mesh=mesh, in_specs=in_specs, out_specs=out_specs, check_vma=False
    )
```

```python
import jax
import jax.numpy as jnp
from jax import lax
from jax.experimental import pallas as pl
from jax.experimental.pallas import tpu as pltpu
from jax.sharding import PartitionSpec as P

BLK = 32
STEPS = 12
ROWS = 256
AXES = ("shot", "rcv")
X, Y, Z, CORES = 4, 4, 4, 2


def moved(value, dx=0, dy=0, dz=0, flip_x=False, flip_core=False):
    def index(x, y, z, core):
        x_hi, x_lo = divmod(x, 2)
        return (((x_hi * Y + y) * 2 + x_lo) * Z + z) * CORES + core

    pairs = []
    for x in range(X):
        for y in range(Y):
            for z in range(Z):
                for core in range(CORES):
                    way = 1 - 2 * core
                    to_x = x ^ 1 if flip_x else (x + way * dx) % X
                    to_core = core ^ 1 if flip_core else core
                    target = index(to_x, (y + way * dy) % Y, (z + way * dz) % Z, to_core)
                    pairs.append((index(x, y, z, core), target))
    return lax.ppermute(value, AXES, pairs)


def choose(refs, which, act):
    if len(refs) == 1:
        act(refs[0])
        return
    half = len(refs) // 2

    @pl.when(which < half)
    def _():
        choose(refs[:half], which, act)

    @pl.when(which >= half)
    def _():
        choose(refs[half:], which - half, act)


def multiply_kernel(a_where, b_where, b_row, *refs):
    a_refs, b_refs = refs[:16], refs[16:24]
    out, a_buf, b_buf, lhs_even, lhs_odd, rhs_even, rhs_odd, a_sem, b_sem = refs[24:]
    freqs = a_buf.shape[1]
    f = pl.program_id(0)
    rcvs = b_buf.shape[4]
    depth = STEPS * 2 * BLK

    def fetch(first_freq, count, slot):
        these = pl.ds(first_freq, count)
        for step in range(STEPS):

            def from_surface(ref):
                pltpu.make_async_copy(
                    ref.at[these], a_buf.at[step, these], a_sem.at[slot]
                ).start()

            choose(a_refs, a_where[step], from_surface)

            def from_traces(ref):
                first = pl.multiple_of(b_row[step], BLK)
                pltpu.make_async_copy(
                    ref.at[these, :, pl.ds(first, BLK)], b_buf.at[step, these], b_sem.at[slot]
                ).start()

            choose(b_refs, b_where[step], from_traces)

    def arrive(first_freq, count, slot):
        these = pl.ds(first_freq, count)
        for buf, sem in ((a_buf, a_sem), (b_buf, b_sem)):
            part = buf.at[:, these]
            pltpu.make_async_copy(part, part, sem.at[slot]).wait()

    def prepare(freq, quarter, lhs, rhs):
        first = quarter * ROWS
        block = a_buf[:, freq, :, :, first : first + ROWS].reshape(depth, ROWS)
        lhs[first : first + ROWS, :] = block.T
        for step in range(quarter * STEPS // 4, (quarter + 1) * STEPS // 4):
            real = b_buf[step, freq, 0]
            imag = b_buf[step, freq, 1]
            rhs[0, step, 0] = real
            rhs[0, step, 1] = -imag
            rhs[1, step, 0] = imag
            rhs[1, step, 1] = real

    def work(lhs, rhs, next_lhs=None, next_rhs=None):
        width = rcvs // 2
        for quarter in range(4):
            part, first = quarter // 2, quarter % 2 * width
            right = rhs[part, :, :, :, first : first + width].reshape(depth, width)
            out[0, part, :, first : first + width] = jnp.dot(
                lhs[...], right, preferred_element_type=jnp.float32
            ).astype(out.dtype)
            if next_lhs is not None:
                prepare(f + 1, quarter, next_lhs, next_rhs)

    @pl.when(f == 0)
    def _():
        fetch(0, 1, 0)
        fetch(1, freqs - 1, 1)
        arrive(0, 1, 0)
        for quarter in range(4):
            prepare(0, quarter, lhs_even, rhs_even)
        arrive(1, freqs - 1, 1)

    @pl.when(f % 2 == 0)
    def _():
        work(lhs_even, rhs_even, lhs_odd, rhs_odd)

    @pl.when((f % 2 == 1) & (f < freqs - 1))
    def _():
        work(lhs_odd, rhs_odd, lhs_even, rhs_even)

    @pl.when(f == freqs - 1)
    def _():
        work(lhs_odd, rhs_odd)


def multiply(a_parts, b_parts, a_where, b_where, b_row):
    freqs, _, _, shots = a_parts[0].shape
    rcvs = b_parts[0].shape[3]
    depth = STEPS * 2 * BLK
    return pl.pallas_call(
        multiply_kernel,
        out_shape=jax.ShapeDtypeStruct((freqs, 2, shots, rcvs), jnp.bfloat16),
        grid_spec=pltpu.PrefetchScalarGridSpec(
            num_scalar_prefetch=3,
            grid=(freqs,),
            in_specs=[pl.BlockSpec(memory_space=pl.ANY)] * (len(a_parts) + len(b_parts)),
            out_specs=pl.BlockSpec((1, 2, shots, rcvs), lambda f, *_: (f, 0, 0, 0)),
            scratch_shapes=[
                pltpu.VMEM((STEPS, freqs, 2, BLK, shots), jnp.bfloat16),
                pltpu.VMEM((STEPS, freqs, 2, BLK, rcvs), jnp.bfloat16),
                pltpu.VMEM((shots, depth), jnp.bfloat16),
                pltpu.VMEM((shots, depth), jnp.bfloat16),
                pltpu.VMEM((2, STEPS, 2, BLK, rcvs), jnp.bfloat16),
                pltpu.VMEM((2, STEPS, 2, BLK, rcvs), jnp.bfloat16),
                pltpu.SemaphoreType.DMA((2,)),
                pltpu.SemaphoreType.DMA((2,)),
            ],
        ),
        compiler_params=pltpu.CompilerParams(vmem_limit_bytes=56 * 1024 * 1024),
        cost_estimate=pl.CostEstimate(
            flops=2 * freqs * shots * 2 * rcvs * depth,
            bytes_accessed=20 * 1024 * 1024,
            transcendentals=0,
        ),
    )(a_where, b_where, b_row, *a_parts, *b_parts)


def places(block_ids):
    shot, rcv = lax.axis_index("shot"), lax.axis_index("rcv")
    core, z, x_lo = rcv % CORES, rcv // CORES % Z, rcv // (CORES * Z)
    of_core, of_z, of_x = block_ids % CORES, block_ids // CORES % Z, block_ids // (CORES * Z)
    distance = jnp.where(of_core == 0, z - of_z, of_z - z) % Z
    a_where = ((of_core != core) * 2 + (of_x != x_lo)) * Z + distance
    owner = block_ids // 2
    y, of_y = shot % Y, owner % Y
    distance = jnp.where(core == 0, y - of_y, of_y - y) % Y
    b_where = (shot // Y != owner // Y) * Y + distance
    return a_where.astype(jnp.int32), b_where.astype(jnp.int32), block_ids % 2 * BLK


def after(value, *earlier):
    return lax.optimization_barrier((value, *earlier))[0]


def per_device(surface_data, source_traces, block_ids):
    a, b = surface_data, source_traces

    def send(name, value, **way):
        with jax.named_scope(name):
            return moved(value, **way)

    def swap(name, value):
        return send(name, value, flip_core=True)

    a_1 = send("a_1", a, dz=1)
    b_x = send("b_x", b, dx=2)
    a_3 = send("a_3", a, dz=-1)
    b_3 = send("b_3", b, dy=-1)
    b_1 = send("b_1", b, dy=1)
    a_x = send("a_x", after(a, a_1), flip_x=True)
    b_x1 = send("b_x1", b_x, dy=1)
    other = swap("other", after(a, a_3))
    a_2 = send("a_2", after(a_1, b_3), dz=1)
    b_2 = send("b_2", b_1, dy=1)
    other_3 = swap("other_3", after(a_3, a_x))
    other_x = swap("other_x", after(a_x, b_x1))
    a_x1 = send("a_x1", after(a_x, other), dz=1)
    a_x2 = send("a_x2", a_2, flip_x=True)
    b_x3 = send("b_x3", after(b_x, b_2), dy=-1)
    a_x3 = send("a_x3", after(a_x, other_3), dz=-1)
    b_x2 = send("b_x2", after(b_x1, other_x), dy=1)
    other_x1 = swap("other_x1", a_x1)
    other_1 = swap("other_1", after(a_1, a_x2))
    other_2 = swap("other_2", after(a_2, b_x3))
    other_x3 = swap("other_x3", a_x3)
    other_x2 = swap("other_x2", after(a_x2, b_x2))

    a_parts = [a, a_1, a_2, a_3, a_x, a_x1, a_x2, a_x3]
    a_parts += [other, other_1, other_2, other_3, other_x, other_x1, other_x2, other_x3]
    b_parts = [b, b_1, b_2, b_3, b_x, b_x1, b_x2, b_x3]
    return multiply(a_parts, b_parts, *places(block_ids))


def solution(mesh):
    in_specs = (P(None, None, "rcv", "shot"), P(None, None, "shot", "rcv"), P())
    out_specs = P(None, None, "shot", "rcv")
    return jax.shard_map(
        per_device, mesh=mesh, in_specs=in_specs, out_specs=out_specs, check_vma=False
    )
```

```python
import jax
import jax.numpy as jnp
from jax import lax
from jax.experimental import pallas as pl
from jax.experimental.pallas import tpu as pltpu
from jax.sharding import PartitionSpec as P

BLK = 32
STEPS = 12
ROWS = 256
AXES = ("shot", "rcv")
X, Y, Z, CORES = 4, 4, 4, 2


def moved(value, dx=0, dy=0, dz=0, flip_x=False, flip_core=False):
    def index(x, y, z, core):
        x_hi, x_lo = divmod(x, 2)
        return (((x_hi * Y + y) * 2 + x_lo) * Z + z) * CORES + core

    pairs = []
    for x in range(X):
        for y in range(Y):
            for z in range(Z):
                for core in range(CORES):
                    way = 1 - 2 * core
                    to_x = x ^ 1 if flip_x else (x + way * dx) % X
                    to_core = core ^ 1 if flip_core else core
                    target = index(to_x, (y + way * dy) % Y, (z + way * dz) % Z, to_core)
                    pairs.append((index(x, y, z, core), target))
    return lax.ppermute(value, AXES, pairs)


def choose(refs, which, act):
    if len(refs) == 1:
        act(refs[0])
        return
    half = len(refs) // 2

    @pl.when(which < half)
    def _():
        choose(refs[:half], which, act)

    @pl.when(which >= half)
    def _():
        choose(refs[half:], which - half, act)


def multiply_kernel(a_where, b_where, b_row, *refs):
    a_refs, b_refs = refs[:16], refs[16:24]
    out, a_buf, b_buf, lhs, rhs, a_sem, b_sem = refs[24:]
    freqs = a_buf.shape[1]
    f = pl.program_id(0)
    rcvs = b_buf.shape[4]

    def fetch(first_freq, count, slot):
        these = pl.ds(first_freq, count)

        @pl.loop(0, STEPS)
        def _(step):
            def from_surface(ref):
                pltpu.make_async_copy(
                    ref.at[these], a_buf.at[step, these], a_sem.at[slot]
                ).start()

            choose(a_refs, a_where[step], from_surface)

            def from_traces(ref):
                first = pl.multiple_of(b_row[step], BLK)
                pltpu.make_async_copy(
                    ref.at[these, :, pl.ds(first, BLK)], b_buf.at[step, these], b_sem.at[slot]
                ).start()

            choose(b_refs, b_where[step], from_traces)

    def arrive(first_freq, count, slot):
        these = pl.ds(first_freq, count)
        for buf, sem in ((a_buf, a_sem), (b_buf, b_sem)):
            part = buf.at[:, these]
            pltpu.make_async_copy(part, part, sem.at[slot]).wait()

    @pl.when(f == 0)
    def _():
        fetch(0, 1, 0)
        fetch(1, freqs - 1, 1)
        arrive(0, 1, 0)

    @pl.when(f == 1)
    def _():
        arrive(1, freqs - 1, 1)

    @pl.loop(0, STEPS)
    def _(step):
        real = b_buf[step, f, 0]
        imag = b_buf[step, f, 1]
        rhs[0, step, 0] = real
        rhs[0, step, 1] = -imag
        rhs[1, step, 0] = imag
        rhs[1, step, 1] = real

    depth = STEPS * 2 * BLK

    @pl.loop(0, lhs.shape[0] // ROWS)
    def _(tile):
        rows = pl.ds(pl.multiple_of(tile * ROWS, ROWS), ROWS)
        lhs[rows, :] = a_buf[:, f, :, :, rows].reshape(depth, ROWS).T

    @pl.loop(0, 2)
    def _(part):
        out[0, part] = jnp.dot(
            lhs[...], rhs[part].reshape(depth, rcvs), preferred_element_type=jnp.float32
        ).astype(out.dtype)


def multiply(a_parts, b_parts, a_where, b_where, b_row):
    freqs, _, _, shots = a_parts[0].shape
    rcvs = b_parts[0].shape[3]
    depth = STEPS * 2 * BLK
    return pl.pallas_call(
        multiply_kernel,
        out_shape=jax.ShapeDtypeStruct((freqs, 2, shots, rcvs), jnp.bfloat16),
        grid_spec=pltpu.PrefetchScalarGridSpec(
            num_scalar_prefetch=3,
            grid=(freqs,),
            in_specs=[pl.BlockSpec(memory_space=pl.ANY)] * (len(a_parts) + len(b_parts)),
            out_specs=pl.BlockSpec((1, 2, shots, rcvs), lambda f, *_: (f, 0, 0, 0)),
            scratch_shapes=[
                pltpu.VMEM((STEPS, freqs, 2, BLK, shots), jnp.bfloat16),
                pltpu.VMEM((STEPS, freqs, 2, BLK, rcvs), jnp.bfloat16),
                pltpu.VMEM((shots, depth), jnp.bfloat16),
                pltpu.VMEM((2, STEPS, 2, BLK, rcvs), jnp.bfloat16),
                pltpu.SemaphoreType.DMA((2,)),
                pltpu.SemaphoreType.DMA((2,)),
            ],
        ),
        compiler_params=pltpu.CompilerParams(vmem_limit_bytes=56 * 1024 * 1024),
        cost_estimate=pl.CostEstimate(
            flops=2 * freqs * shots * 2 * rcvs * depth,
            bytes_accessed=20 * 1024 * 1024,
            transcendentals=0,
        ),
    )(a_where, b_where, b_row, *a_parts, *b_parts)


def places(block_ids):
    shot, rcv = lax.axis_index("shot"), lax.axis_index("rcv")
    core, z, x_lo = rcv % CORES, rcv // CORES % Z, rcv // (CORES * Z)
    of_core, of_z, of_x = block_ids % CORES, block_ids // CORES % Z, block_ids // (CORES * Z)
    distance = jnp.where(of_core == 0, z - of_z, of_z - z) % Z
    a_where = ((of_core != core) * 2 + (of_x != x_lo)) * Z + distance
    owner = block_ids // 2
    y, of_y = shot % Y, owner % Y
    distance = jnp.where(core == 0, y - of_y, of_y - y) % Y
    b_where = (shot // Y != owner // Y) * Y + distance
    return a_where.astype(jnp.int32), b_where.astype(jnp.int32), block_ids % 2 * BLK


def after(value, *earlier):
    return lax.optimization_barrier((value, *earlier))[0]


def per_device(surface_data, source_traces, block_ids):
    a, b = surface_data, source_traces

    def send(name, value, **way):
        with jax.named_scope(name):
            return moved(value, **way)

    def swap(name, value):
        return send(name, value, flip_core=True)

    b_3 = send("b_3", b, dy=-1)
    b_x = send("b_x", b, dx=2)
    a_3 = send("a_3", a, dz=-1)
    b_1 = send("b_1", b, dy=1)
    a_1 = send("a_1", a, dz=1)
    a_x = send("a_x", after(a, b_3), flip_x=True)
    other_3 = swap("other_3", after(a_3, b_x))
    b_x1 = send("b_x1", after(b_x, a_3), dy=1)
    a_2 = send("a_2", after(a_1, b_1), dz=1)
    b_x3 = send("b_x3", after(b_x, a_1), dy=-1)
    a_x3 = send("a_x3", a_x, dz=-1)
    b_2 = send("b_2", after(b_1, other_3), dy=1)
    a_x2 = send("a_x2", after(a_2, b_x1), flip_x=True)
    b_x2 = send("b_x2", after(b_x1, a_2), dy=1)
    a_x1 = send("a_x1", after(a_x, b_x3), dz=1)
    other = swap("other", after(a, a_x3))
    other_2 = swap("other_2", after(a_2, b_2))
    other_1 = swap("other_1", after(a_1, a_x2))
    other_x2 = swap("other_x2", after(a_x2, b_x2))
    other_x1 = swap("other_x1", a_x1)
    other_x = swap("other_x", after(a_x, other))
    other_x3 = swap("other_x3", after(a_x3, other_2))

    a_parts = [a, a_1, a_2, a_3, a_x, a_x1, a_x2, a_x3]
    a_parts += [other, other_1, other_2, other_3, other_x, other_x1, other_x2, other_x3]
    b_parts = [b, b_1, b_2, b_3, b_x, b_x1, b_x2, b_x3]
    return multiply(a_parts, b_parts, *places(block_ids))


def solution(mesh):
    in_specs = (P(None, None, "rcv", "shot"), P(None, None, "shot", "rcv"), P())
    out_specs = P(None, None, "shot", "rcv")
    return jax.shard_map(
        per_device, mesh=mesh, in_specs=in_specs, out_specs=out_specs, check_vma=False
    )
```

```python
import jax
import jax.numpy as jnp
from jax import lax
from jax.experimental import pallas as pl
from jax.experimental.pallas import tpu as pltpu
from jax.sharding import PartitionSpec as P

BLK = 32
STEPS = 12
ROWS = 256
AXES = ("shot", "rcv")
X, Y, Z, CORES = 4, 4, 4, 2


def moved(value, dx=0, dy=0, dz=0, flip_x=False, flip_core=False):
    def index(x, y, z, core):
        x_hi, x_lo = divmod(x, 2)
        return (((x_hi * Y + y) * 2 + x_lo) * Z + z) * CORES + core

    pairs = []
    for x in range(X):
        for y in range(Y):
            for z in range(Z):
                for core in range(CORES):
                    way = 1 - 2 * core
                    to_x = x ^ 1 if flip_x else (x + way * dx) % X
                    to_core = core ^ 1 if flip_core else core
                    target = index(to_x, (y + way * dy) % Y, (z + way * dz) % Z, to_core)
                    pairs.append((index(x, y, z, core), target))
    return lax.ppermute(value, AXES, pairs)


def choose(refs, which, act):
    if len(refs) == 1:
        act(refs[0])
        return
    half = len(refs) // 2

    @pl.when(which < half)
    def _():
        choose(refs[:half], which, act)

    @pl.when(which >= half)
    def _():
        choose(refs[half:], which - half, act)


def multiply_kernel(a_where, b_where, b_row, *refs):
    a_refs, b_refs = refs[:16], refs[16:24]
    out, a_buf, b_buf, lhs, rhs, a_sem, b_sem = refs[24:]
    freqs = a_buf.shape[1]
    f = pl.program_id(0)
    rcvs = b_buf.shape[4]

    def fetch(first_freq, count, slot):
        these = pl.ds(first_freq, count)

        @pl.loop(0, STEPS)
        def _(step):
            def from_surface(ref):
                pltpu.make_async_copy(
                    ref.at[these], a_buf.at[step, these], a_sem.at[slot]
                ).start()

            choose(a_refs, a_where[step], from_surface)

            def from_traces(ref):
                first = pl.multiple_of(b_row[step], BLK)
                pltpu.make_async_copy(
                    ref.at[these, :, pl.ds(first, BLK)], b_buf.at[step, these], b_sem.at[slot]
                ).start()

            choose(b_refs, b_where[step], from_traces)

    def arrive(first_freq, count, slot):
        these = pl.ds(first_freq, count)
        for buf, sem in ((a_buf, a_sem), (b_buf, b_sem)):
            part = buf.at[:, these]
            pltpu.make_async_copy(part, part, sem.at[slot]).wait()

    @pl.when(f == 0)
    def _():
        fetch(0, 1, 0)
        fetch(1, freqs - 1, 1)
        arrive(0, 1, 0)

    @pl.when(f == 1)
    def _():
        arrive(1, freqs - 1, 1)

    for step in range(STEPS):
        real = b_buf[step, f, 0]
        imag = b_buf[step, f, 1]
        rhs[0, step, 0] = real
        rhs[0, step, 1] = -imag
        rhs[1, step, 0] = imag
        rhs[1, step, 1] = real

    depth = STEPS * 2 * BLK
    for first in range(0, lhs.shape[0], ROWS):
        block = a_buf[:, f, :, :, first : first + ROWS].reshape(depth, ROWS)
        lhs[first : first + ROWS, :] = block.T

    for part in range(2):
        out[0, part] = jnp.dot(
            lhs[...], rhs[part].reshape(depth, rcvs), preferred_element_type=jnp.float32
        ).astype(out.dtype)


def multiply(a_parts, b_parts, a_where, b_where, b_row):
    freqs, _, _, shots = a_parts[0].shape
    rcvs = b_parts[0].shape[3]
    depth = STEPS * 2 * BLK
    return pl.pallas_call(
        multiply_kernel,
        out_shape=jax.ShapeDtypeStruct((freqs, 2, shots, rcvs), jnp.bfloat16),
        grid_spec=pltpu.PrefetchScalarGridSpec(
            num_scalar_prefetch=3,
            grid=(freqs,),
            in_specs=[pl.BlockSpec(memory_space=pl.ANY)] * (len(a_parts) + len(b_parts)),
            out_specs=pl.BlockSpec((1, 2, shots, rcvs), lambda f, *_: (f, 0, 0, 0)),
            scratch_shapes=[
                pltpu.VMEM((STEPS, freqs, 2, BLK, shots), jnp.bfloat16),
                pltpu.VMEM((STEPS, freqs, 2, BLK, rcvs), jnp.bfloat16),
                pltpu.VMEM((shots, depth), jnp.bfloat16),
                pltpu.VMEM((2, STEPS, 2, BLK, rcvs), jnp.bfloat16),
                pltpu.SemaphoreType.DMA((2,)),
                pltpu.SemaphoreType.DMA((2,)),
            ],
        ),
        compiler_params=pltpu.CompilerParams(vmem_limit_bytes=56 * 1024 * 1024),
        cost_estimate=pl.CostEstimate(
            flops=2 * freqs * shots * 2 * rcvs * depth,
            bytes_accessed=20 * 1024 * 1024,
            transcendentals=0,
        ),
    )(a_where, b_where, b_row, *a_parts, *b_parts)


def places(block_ids):
    shot, rcv = lax.axis_index("shot"), lax.axis_index("rcv")
    core, z, x_lo = rcv % CORES, rcv // CORES % Z, rcv // (CORES * Z)
    of_core, of_z, of_x = block_ids % CORES, block_ids // CORES % Z, block_ids // (CORES * Z)
    distance = jnp.where(of_core == 0, z - of_z, of_z - z) % Z
    a_where = ((of_core != core) * 2 + (of_x != x_lo)) * Z + distance
    owner = block_ids // 2
    y, of_y = shot % Y, owner % Y
    distance = jnp.where(core == 0, y - of_y, of_y - y) % Y
    b_where = (shot // Y != owner // Y) * Y + distance
    return a_where.astype(jnp.int32), b_where.astype(jnp.int32), block_ids % 2 * BLK


def after(value, *earlier):
    return lax.optimization_barrier((value, *earlier))[0]


def per_device(surface_data, source_traces, block_ids):
    a, b = surface_data, source_traces
    a_where, b_where, b_row = places(block_ids)

    def send(name, value, **way):
        with jax.named_scope(name):
            return moved(value, **way)

    def swap(name, value):
        return send(name, value, flip_core=True)

    b_3 = send("b_3", b, dy=-1)
    b_x = send("b_x", b, dx=2)
    a_3 = send("a_3", a, dz=-1)
    b_1 = send("b_1", b, dy=1)
    a_1 = send("a_1", a, dz=1)
    a_x = send("a_x", after(a, b_3, a_where, b_where, b_row), flip_x=True)
    other_3 = swap("other_3", after(a_3, b_x))
    b_x1 = send("b_x1", after(b_x, a_3), dy=1)
    a_2 = send("a_2", after(a_1, b_1), dz=1)
    b_x3 = send("b_x3", after(b_x, a_1), dy=-1)
    a_x3 = send("a_x3", a_x, dz=-1)
    b_2 = send("b_2", after(b_1, other_3), dy=1)
    a_x2 = send("a_x2", after(a_2, b_x1), flip_x=True)
    b_x2 = send("b_x2", after(b_x1, a_2), dy=1)
    a_x1 = send("a_x1", after(a_x, b_x3), dz=1)
    other = swap("other", after(a, a_x3))
    other_2 = swap("other_2", after(a_2, b_2))
    other_1 = swap("other_1", after(a_1, a_x2))
    other_x2 = swap("other_x2", after(a_x2, b_x2))
    other_x1 = swap("other_x1", a_x1)
    other_x = swap("other_x", after(a_x, other))
    other_x3 = swap("other_x3", after(a_x3, other_2))

    a_parts = [a, a_1, a_2, a_3, a_x, a_x1, a_x2, a_x3]
    a_parts += [other, other_1, other_2, other_3, other_x, other_x1, other_x2, other_x3]
    b_parts = [b, b_1, b_2, b_3, b_x, b_x1, b_x2, b_x3]
    return multiply(a_parts, b_parts, a_where, b_where, b_row)


def solution(mesh):
    in_specs = (P(None, None, "rcv", "shot"), P(None, None, "shot", "rcv"), P())
    out_specs = P(None, None, "shot", "rcv")
    return jax.shard_map(
        per_device, mesh=mesh, in_specs=in_specs, out_specs=out_specs, check_vma=False
    )
```

```python
import jax
import jax.numpy as jnp
from jax import lax
from jax.experimental import pallas as pl
from jax.experimental.pallas import tpu as pltpu
from jax.sharding import PartitionSpec as P

BLK = 32
STEPS = 12
ROWS = 256
AXES = ("shot", "rcv")
X, Y, Z, CORES = 4, 4, 4, 2


def moved(value, dx=0, dy=0, dz=0, flip_x=False, flip_core=False):
    def index(x, y, z, core):
        x_hi, x_lo = divmod(x, 2)
        return (((x_hi * Y + y) * 2 + x_lo) * Z + z) * CORES + core

    pairs = []
    for x in range(X):
        for y in range(Y):
            for z in range(Z):
                for core in range(CORES):
                    way = 1 - 2 * core
                    to_x = x ^ 1 if flip_x else (x + way * dx) % X
                    to_core = core ^ 1 if flip_core else core
                    target = index(to_x, (y + way * dy) % Y, (z + way * dz) % Z, to_core)
                    pairs.append((index(x, y, z, core), target))
    return lax.ppermute(value, AXES, pairs)


def choose(refs, which, act):
    if len(refs) == 1:
        act(refs[0])
        return
    half = len(refs) // 2

    @pl.when(which < half)
    def _():
        choose(refs[:half], which, act)

    @pl.when(which >= half)
    def _():
        choose(refs[half:], which - half, act)


def transpose_kernel(block, out):
    for pair in range(out.shape[0]):
        rows = block[2 * pair : 2 * pair + 2].reshape(4 * BLK, block.shape[3])
        out[pair] = rows.T


def transposed(block):
    freqs, _, _, shots = block.shape
    return pl.pallas_call(
        transpose_kernel,
        out_shape=jax.ShapeDtypeStruct((freqs // 2, shots, 4 * BLK), block.dtype),
        in_specs=[pl.BlockSpec(memory_space=pltpu.VMEM)],
        out_specs=pl.BlockSpec(memory_space=pltpu.VMEM),
        cost_estimate=pl.CostEstimate(
            flops=0, bytes_accessed=2 * block.size * 2, transcendentals=0
        ),
    )(block)


def multiply_kernel(a_where, b_where, b_row, *refs):
    a_refs, b_refs = refs[:16], refs[16:24]
    out, a_buf, b_buf, lhs, rhs, a_sem, b_sem = refs[24:]
    f = pl.program_id(0)
    pair, second = f // 2, f % 2
    rcvs = b_buf.shape[4]

    def fetch(slot):
        these = pl.ds(2 * slot, 2)
        for step in range(STEPS):

            def from_surface(ref):
                pltpu.make_async_copy(
                    ref.at[slot], a_buf.at[slot, step], a_sem.at[slot]
                ).start()

            choose(a_refs, a_where[step], from_surface)

            def from_traces(ref):
                first = pl.multiple_of(b_row[step], BLK)
                pltpu.make_async_copy(
                    ref.at[these, :, pl.ds(first, BLK)], b_buf.at[step, these], b_sem.at[slot]
                ).start()

            choose(b_refs, b_where[step], from_traces)

    def arrive(slot):
        for part, sem in ((a_buf.at[slot], a_sem), (b_buf.at[:, pl.ds(2 * slot, 2)], b_sem)):
            pltpu.make_async_copy(part, part, sem.at[slot]).wait()

    @pl.when(f == 0)
    def _():
        fetch(0)
        fetch(1)
        arrive(0)

    @pl.when(f == 2)
    def _():
        arrive(1)

    for step in range(STEPS):
        real = b_buf[step, f, 0]
        imag = b_buf[step, f, 1]
        rhs[0, step, 0] = real
        rhs[0, step, 1] = -imag
        rhs[1, step, 0] = imag
        rhs[1, step, 1] = real

    depth = STEPS * 2 * BLK
    columns = 4 * BLK
    lane = lax.broadcasted_iota(jnp.int32, (lhs.shape[0], columns), 1)
    for chunk in range(STEPS // 2):
        left = pltpu.roll(a_buf[pair, 2 * chunk], second * (columns // 2), 1)
        right = pltpu.roll(a_buf[pair, 2 * chunk + 1], (1 - second) * (columns // 2), 1)
        joined = jnp.where(lane < columns // 2, left, right)
        lhs[:, chunk * columns : (chunk + 1) * columns] = joined

    for part in range(2):
        out[0, part] = jnp.dot(
            lhs[...], rhs[part].reshape(depth, rcvs), preferred_element_type=jnp.float32
        ).astype(out.dtype)


def multiply(a_parts, b_parts, a_where, b_where, b_row):
    pairs, shots, columns = a_parts[0].shape
    freqs, _, _, rcvs = b_parts[0].shape
    depth = STEPS * 2 * BLK
    return pl.pallas_call(
        multiply_kernel,
        out_shape=jax.ShapeDtypeStruct((freqs, 2, shots, rcvs), jnp.bfloat16),
        grid_spec=pltpu.PrefetchScalarGridSpec(
            num_scalar_prefetch=3,
            grid=(freqs,),
            in_specs=[pl.BlockSpec(memory_space=pl.ANY)] * (len(a_parts) + len(b_parts)),
            out_specs=pl.BlockSpec((1, 2, shots, rcvs), lambda f, *_: (f, 0, 0, 0)),
            scratch_shapes=[
                pltpu.VMEM((pairs, STEPS, shots, columns), jnp.bfloat16),
                pltpu.VMEM((STEPS, freqs, 2, BLK, rcvs), jnp.bfloat16),
                pltpu.VMEM((shots, depth), jnp.bfloat16),
                pltpu.VMEM((2, STEPS, 2, BLK, rcvs), jnp.bfloat16),
                pltpu.SemaphoreType.DMA((2,)),
                pltpu.SemaphoreType.DMA((2,)),
            ],
        ),
        compiler_params=pltpu.CompilerParams(vmem_limit_bytes=56 * 1024 * 1024),
        cost_estimate=pl.CostEstimate(
            flops=2 * freqs * shots * 2 * rcvs * depth,
            bytes_accessed=20 * 1024 * 1024,
            transcendentals=0,
        ),
    )(a_where, b_where, b_row, *a_parts, *b_parts)


def places(block_ids):
    shot, rcv = lax.axis_index("shot"), lax.axis_index("rcv")
    core, z, x_lo = rcv % CORES, rcv // CORES % Z, rcv // (CORES * Z)
    of_core, of_z, of_x = block_ids % CORES, block_ids // CORES % Z, block_ids // (CORES * Z)
    distance = jnp.where(of_core == 0, z - of_z, of_z - z) % Z
    a_where = ((of_core != core) * 2 + (of_x != x_lo)) * Z + distance
    owner = block_ids // 2
    y, of_y = shot % Y, owner % Y
    distance = jnp.where(core == 0, y - of_y, of_y - y) % Y
    b_where = (shot // Y != owner // Y) * Y + distance
    return a_where.astype(jnp.int32), b_where.astype(jnp.int32), block_ids % 2 * BLK


def after(value, *earlier):
    return lax.optimization_barrier((value, *earlier))[0]


def per_device(surface_data, source_traces, block_ids):
    a, b = transposed(surface_data), source_traces
    a_where, b_where, b_row = places(block_ids)

    def send(name, value, **way):
        with jax.named_scope(name):
            return moved(value, **way)

    def swap(name, value):
        return send(name, value, flip_core=True)

    b_3 = send("b_3", b, dy=-1)
    b_x = send("b_x", b, dx=2)
    a_3 = send("a_3", a, dz=-1)
    b_1 = send("b_1", b, dy=1)
    a_1 = send("a_1", a, dz=1)
    a_x = send("a_x", after(a, b_3, a_where, b_where, b_row), flip_x=True)
    other_3 = swap("other_3", after(a_3, b_x))
    b_x1 = send("b_x1", after(b_x, a_3), dy=1)
    a_2 = send("a_2", after(a_1, b_1), dz=1)
    b_x3 = send("b_x3", after(b_x, a_1), dy=-1)
    b_2 = send("b_2", after(b_1, a_x), dy=1)
    a_x3 = send("a_x3", after(a_x, other_3, b_x1), dz=-1)
    a_x2 = send("a_x2", after(a_2, b_x1), flip_x=True)
    b_x2 = send("b_x2", after(b_x1, a_2), dy=1)
    a_x1 = send("a_x1", after(a_x, b_x3), dz=1)
    other_2 = swap("other_2", after(a_2, b_2))
    other_1 = swap("other_1", after(a_1, a_x3))
    other_x2 = swap("other_x2", a_x2)
    other = swap("other", after(a, b_x2))
    other_x1 = swap("other_x1", a_x1)
    other_x3 = swap("other_x3", after(a_x3, other_2))
    other_x = swap("other_x", after(a_x, other_1))

    a_parts = [a, a_1, a_2, a_3, a_x, a_x1, a_x2, a_x3]
    a_parts += [other, other_1, other_2, other_3, other_x, other_x1, other_x2, other_x3]
    b_parts = [b, b_1, b_2, b_3, b_x, b_x1, b_x2, b_x3]
    return multiply(a_parts, b_parts, a_where, b_where, b_row)


def solution(mesh):
    in_specs = (P(None, None, "rcv", "shot"), P(None, None, "shot", "rcv"), P())
    out_specs = P(None, None, "shot", "rcv")
    return jax.shard_map(
        per_device, mesh=mesh, in_specs=in_specs, out_specs=out_specs, check_vma=False
    )
```

```python
import jax
import jax.numpy as jnp
from jax import lax
from jax.experimental import pallas as pl
from jax.experimental.pallas import tpu as pltpu
from jax.sharding import PartitionSpec as P

BLK = 32
STEPS = 12
ROWS = 256
AXES = ("shot", "rcv")
X, Y, Z, CORES = 4, 4, 4, 2


def moved(value, dx=0, dy=0, dz=0, flip_x=False, flip_core=False):
    def index(x, y, z, core):
        x_hi, x_lo = divmod(x, 2)
        return (((x_hi * Y + y) * 2 + x_lo) * Z + z) * CORES + core

    pairs = []
    for x in range(X):
        for y in range(Y):
            for z in range(Z):
                for core in range(CORES):
                    way = 1 - 2 * core
                    to_x = x ^ 1 if flip_x else (x + way * dx) % X
                    to_core = core ^ 1 if flip_core else core
                    target = index(to_x, (y + way * dy) % Y, (z + way * dz) % Z, to_core)
                    pairs.append((index(x, y, z, core), target))
    return lax.ppermute(value, AXES, pairs)


def choose(refs, which, act):
    if len(refs) == 1:
        act(refs[0])
        return
    half = len(refs) // 2

    @pl.when(which < half)
    def _():
        choose(refs[:half], which, act)

    @pl.when(which >= half)
    def _():
        choose(refs[half:], which - half, act)


def multiply_kernel(a_where, b_where, b_row, *refs):
    a_refs, b_refs = refs[:16], refs[16:24]
    out, a_buf, b_buf, lhs, rhs, a_sem, b_sem = refs[24:]
    freqs = a_buf.shape[1]
    f = pl.program_id(0)
    rcvs = b_buf.shape[4]

    def fetch(first_freq, count, slot):
        these = pl.ds(first_freq, count)
        for step in range(STEPS):

            def from_surface(ref):
                pltpu.make_async_copy(
                    ref.at[these], a_buf.at[step, these], a_sem.at[slot]
                ).start()

            choose(a_refs, a_where[step], from_surface)

            def from_traces(ref):
                first = pl.multiple_of(b_row[step], BLK)
                pltpu.make_async_copy(
                    ref.at[these, :, pl.ds(first, BLK)], b_buf.at[step, these], b_sem.at[slot]
                ).start()

            choose(b_refs, b_where[step], from_traces)

    def arrive(first_freq, count, slot):
        these = pl.ds(first_freq, count)
        for buf, sem in ((a_buf, a_sem), (b_buf, b_sem)):
            part = buf.at[:, these]
            pltpu.make_async_copy(part, part, sem.at[slot]).wait()

    @pl.when(f == 0)
    def _():
        fetch(0, 1, 0)
        fetch(1, freqs - 1, 1)
        arrive(0, 1, 0)

    @pl.when(f == 1)
    def _():
        arrive(1, freqs - 1, 1)

    for step in range(STEPS):
        real = b_buf[step, f, 0]
        imag = b_buf[step, f, 1]
        rhs[step, 0, :, :rcvs] = real
        rhs[step, 0, :, rcvs:] = imag
        rhs[step, 1, :, :rcvs] = -imag
        rhs[step, 1, :, rcvs:] = real

    depth = STEPS * 2 * BLK
    for first in range(0, lhs.shape[0], ROWS):
        block = a_buf[:, f, :, :, first : first + ROWS].reshape(depth, ROWS)
        lhs[first : first + ROWS, :] = block.T

    product = jnp.dot(
        lhs[...], rhs[...].reshape(depth, 2 * rcvs), preferred_element_type=jnp.float32
    ).astype(out.dtype)
    out[0, 0] = product[:, :rcvs]
    out[0, 1] = product[:, rcvs:]


def multiply(a_parts, b_parts, a_where, b_where, b_row):
    freqs, _, _, shots = a_parts[0].shape
    rcvs = b_parts[0].shape[3]
    depth = STEPS * 2 * BLK
    return pl.pallas_call(
        multiply_kernel,
        out_shape=jax.ShapeDtypeStruct((freqs, 2, shots, rcvs), jnp.bfloat16),
        grid_spec=pltpu.PrefetchScalarGridSpec(
            num_scalar_prefetch=3,
            grid=(freqs,),
            in_specs=[pl.BlockSpec(memory_space=pl.ANY)] * (len(a_parts) + len(b_parts)),
            out_specs=pl.BlockSpec((1, 2, shots, rcvs), lambda f, *_: (f, 0, 0, 0)),
            scratch_shapes=[
                pltpu.VMEM((STEPS, freqs, 2, BLK, shots), jnp.bfloat16),
                pltpu.VMEM((STEPS, freqs, 2, BLK, rcvs), jnp.bfloat16),
                pltpu.VMEM((shots, depth), jnp.bfloat16),
                pltpu.VMEM((STEPS, 2, BLK, 2 * rcvs), jnp.bfloat16),
                pltpu.SemaphoreType.DMA((2,)),
                pltpu.SemaphoreType.DMA((2,)),
            ],
        ),
        compiler_params=pltpu.CompilerParams(vmem_limit_bytes=56 * 1024 * 1024),
        cost_estimate=pl.CostEstimate(
            flops=2 * freqs * shots * 2 * rcvs * depth,
            bytes_accessed=20 * 1024 * 1024,
            transcendentals=0,
        ),
    )(a_where, b_where, b_row, *a_parts, *b_parts)


def places(block_ids):
    shot, rcv = lax.axis_index("shot"), lax.axis_index("rcv")
    core, z, x_lo = rcv % CORES, rcv // CORES % Z, rcv // (CORES * Z)
    of_core, of_z, of_x = block_ids % CORES, block_ids // CORES % Z, block_ids // (CORES * Z)
    distance = jnp.where(of_core == 0, z - of_z, of_z - z) % Z
    a_where = ((of_core != core) * 2 + (of_x != x_lo)) * Z + distance
    owner = block_ids // 2
    y, of_y = shot % Y, owner % Y
    distance = jnp.where(core == 0, y - of_y, of_y - y) % Y
    b_where = (shot // Y != owner // Y) * Y + distance
    return a_where.astype(jnp.int32), b_where.astype(jnp.int32), block_ids % 2 * BLK


def after(value, *earlier):
    return lax.optimization_barrier((value, *earlier))[0]


def per_device(surface_data, source_traces, block_ids):
    a, b = surface_data, source_traces
    a_where, b_where, b_row = places(block_ids)

    def send(name, value, **way):
        with jax.named_scope(name):
            return moved(value, **way)

    def swap(name, value):
        return send(name, value, flip_core=True)

    b_3 = send("b_3", b, dy=-1)
    b_x = send("b_x", b, dx=2)
    a_3 = send("a_3", a, dz=-1)
    b_1 = send("b_1", b, dy=1)
    a_1 = send("a_1", a, dz=1)
    a_x = send("a_x", after(a, b_3, a_where, b_where, b_row), flip_x=True)
    other_3 = swap("other_3", after(a_3, b_x))
    b_x1 = send("b_x1", after(b_x, a_3), dy=1)
    a_2 = send("a_2", after(a_1, b_1), dz=1)
    b_x3 = send("b_x3", after(b_x, a_1), dy=-1)
    b_2 = send("b_2", after(b_1, a_x), dy=1)
    a_x3 = send("a_x3", after(a_x, other_3, b_x1), dz=-1)
    a_x2 = send("a_x2", after(a_2, b_x1), flip_x=True)
    b_x2 = send("b_x2", after(b_x1, a_2), dy=1)
    a_x1 = send("a_x1", after(a_x, b_x3), dz=1)
    other_2 = swap("other_2", after(a_2, b_2))
    other_1 = swap("other_1", after(a_1, a_x3))
    other_x2 = swap("other_x2", a_x2)
    other = swap("other", after(a, b_x2))
    other_x1 = swap("other_x1", a_x1)
    other_x3 = swap("other_x3", after(a_x3, other_2))
    other_x = swap("other_x", after(a_x, other_1))

    a_parts = [a, a_1, a_2, a_3, a_x, a_x1, a_x2, a_x3]
    a_parts += [other, other_1, other_2, other_3, other_x, other_x1, other_x2, other_x3]
    b_parts = [b, b_1, b_2, b_3, b_x, b_x1, b_x2, b_x3]
    return multiply(a_parts, b_parts, a_where, b_where, b_row)


def solution(mesh):
    in_specs = (P(None, None, "rcv", "shot"), P(None, None, "shot", "rcv"), P())
    out_specs = P(None, None, "shot", "rcv")
    return jax.shard_map(
        per_device, mesh=mesh, in_specs=in_specs, out_specs=out_specs, check_vma=False
    )
```

```python
import jax
import jax.numpy as jnp
from jax import lax
from jax.experimental import pallas as pl
from jax.experimental.pallas import tpu as pltpu
from jax.sharding import PartitionSpec as P

BLK = 32
STEPS = 12
ROWS = 256
AXES = ("shot", "rcv")
X, Y, Z, CORES = 4, 4, 4, 2


def moved(value, dx=0, dy=0, dz=0, flip_x=False, flip_core=False):
    def index(x, y, z, core):
        x_hi, x_lo = divmod(x, 2)
        return (((x_hi * Y + y) * 2 + x_lo) * Z + z) * CORES + core

    pairs = []
    for x in range(X):
        for y in range(Y):
            for z in range(Z):
                for core in range(CORES):
                    way = 1 - 2 * core
                    to_x = x ^ 1 if flip_x else (x + way * dx) % X
                    to_core = core ^ 1 if flip_core else core
                    target = index(to_x, (y + way * dy) % Y, (z + way * dz) % Z, to_core)
                    pairs.append((index(x, y, z, core), target))
    return lax.ppermute(value, AXES, pairs)


def choose(refs, which, act):
    if len(refs) == 1:
        act(refs[0])
        return
    half = len(refs) // 2

    @pl.when(which < half)
    def _():
        choose(refs[:half], which, act)

    @pl.when(which >= half)
    def _():
        choose(refs[half:], which - half, act)


def multiply_kernel(a_where, b_where, b_row, *refs):
    a_refs, b_refs = refs[:16], refs[16:24]
    out, a_buf, b_buf, lhs, rhs, a_sem, b_sem = refs[24:]
    freqs = a_buf.shape[1]
    f = pl.program_id(0)
    rcvs = b_buf.shape[4]

    def fetch(first_freq, count, slot):
        these = pl.ds(first_freq, count)
        for step in range(STEPS):

            def from_surface(ref):
                pltpu.make_async_copy(
                    ref.at[these], a_buf.at[step, these], a_sem.at[slot]
                ).start()

            choose(a_refs, a_where[step], from_surface)

            def from_traces(ref):
                first = pl.multiple_of(b_row[step], BLK)
                pltpu.make_async_copy(
                    ref.at[these, :, pl.ds(first, BLK)], b_buf.at[step, these], b_sem.at[slot]
                ).start()

            choose(b_refs, b_where[step], from_traces)

    def arrive(first_freq, count, slot):
        these = pl.ds(first_freq, count)
        for buf, sem in ((a_buf, a_sem), (b_buf, b_sem)):
            part = buf.at[:, these]
            pltpu.make_async_copy(part, part, sem.at[slot]).wait()

    @pl.when(f == 0)
    def _():
        fetch(0, 1, 0)
        fetch(1, freqs - 1, 1)
        arrive(0, 1, 0)

    @pl.when(f == 1)
    def _():
        arrive(1, freqs - 1, 1)

    for step in range(STEPS):
        real = b_buf[step, f, 0]
        imag = b_buf[step, f, 1]
        rhs[step, 0, :, :rcvs] = real
        rhs[step, 0, :, rcvs:] = imag
        rhs[step, 1, :, :rcvs] = -imag
        rhs[step, 1, :, rcvs:] = real

    depth = STEPS * 2 * BLK
    for first in range(0, lhs.shape[0], ROWS):
        block = a_buf[:, f, :, :, first : first + ROWS].reshape(depth, ROWS)
        lhs[first : first + ROWS, :] = block.T

    product = jnp.dot(
        lhs[...], rhs[...].reshape(depth, 2 * rcvs), preferred_element_type=jnp.float32
    ).astype(out.dtype)
    out[0, 0] = product[:, :rcvs]
    out[0, 1] = product[:, rcvs:]


def multiply(a_parts, b_parts, a_where, b_where, b_row):
    freqs, _, _, shots = a_parts[0].shape
    rcvs = b_parts[0].shape[3]
    depth = STEPS * 2 * BLK
    return pl.pallas_call(
        multiply_kernel,
        out_shape=jax.ShapeDtypeStruct((freqs, 2, shots, rcvs), jnp.bfloat16),
        grid_spec=pltpu.PrefetchScalarGridSpec(
            num_scalar_prefetch=3,
            grid=(freqs,),
            in_specs=[pl.BlockSpec(memory_space=pl.ANY)] * (len(a_parts) + len(b_parts)),
            out_specs=pl.BlockSpec((1, 2, shots, rcvs), lambda f, *_: (f, 0, 0, 0)),
            scratch_shapes=[
                pltpu.VMEM((STEPS, freqs, 2, BLK, shots), jnp.bfloat16),
                pltpu.VMEM((STEPS, freqs, 2, BLK, rcvs), jnp.bfloat16),
                pltpu.VMEM((shots, depth), jnp.bfloat16),
                pltpu.VMEM((STEPS, 2, BLK, 2 * rcvs), jnp.bfloat16),
                pltpu.SemaphoreType.DMA((2,)),
                pltpu.SemaphoreType.DMA((2,)),
            ],
        ),
        compiler_params=pltpu.CompilerParams(vmem_limit_bytes=56 * 1024 * 1024),
        cost_estimate=pl.CostEstimate(
            flops=2 * freqs * shots * 2 * rcvs * depth,
            bytes_accessed=20 * 1024 * 1024,
            transcendentals=0,
        ),
    )(a_where, b_where, b_row, *a_parts, *b_parts)


def places(block_ids):
    shot, rcv = lax.axis_index("shot"), lax.axis_index("rcv")
    core, z, x_lo = rcv % CORES, rcv // CORES % Z, rcv // (CORES * Z)
    of_core, of_z, of_x = block_ids % CORES, block_ids // CORES % Z, block_ids // (CORES * Z)
    distance = jnp.where(of_core == 0, z - of_z, of_z - z) % Z
    a_where = ((of_core != core) * 2 + (of_x != x_lo)) * Z + distance
    owner = block_ids // 2
    y, of_y = shot % Y, owner % Y
    distance = jnp.where(core == 0, y - of_y, of_y - y) % Y
    b_where = (shot // Y != owner // Y) * Y + distance
    return a_where.astype(jnp.int32), b_where.astype(jnp.int32), block_ids % 2 * BLK


def after(value, *earlier):
    return lax.optimization_barrier((value, *earlier))[0]


def per_device(surface_data, source_traces, block_ids):
    a, b = surface_data, source_traces
    a_where, b_where, b_row = places(block_ids)

    def send(name, value, **way):
        with jax.named_scope(name):
            return moved(value, **way)

    def swap(name, value):
        return send(name, value, flip_core=True)

    b_3 = send("b_3", b, dy=-1)
    b_x = send("b_x", b, dx=2)
    a_3 = send("a_3", a, dz=-1)
    b_1 = send("b_1", b, dy=1)
    a_1 = send("a_1", a, dz=1)
    a_x = send("a_x", after(a, b_3, a_where, b_where, b_row), flip_x=True)
    other_3 = swap("other_3", after(a_3, b_x))
    b_x1 = send("b_x1", after(b_x, a_3), dy=1)
    a_2 = send("a_2", after(a_1, b_1), dz=1)
    b_x3 = send("b_x3", after(b_x, a_1), dy=-1)
    a_x3 = send("a_x3", a_x, dz=-1)
    b_2 = send("b_2", after(b_1, other_3), dy=1)
    a_x2 = send("a_x2", after(a_2, b_x1), flip_x=True)
    b_x2 = send("b_x2", after(b_x1, a_2), dy=1)
    a_x1 = send("a_x1", after(a_x, b_x3), dz=1)
    other = swap("other", after(a, a_x3))
    other_2 = swap("other_2", after(a_2, b_2))
    other_1 = swap("other_1", after(a_1, a_x2))
    other_x2 = swap("other_x2", after(a_x2, b_x2))
    other_x1 = swap("other_x1", a_x1)
    other_x = swap("other_x", after(a_x, other))
    other_x3 = swap("other_x3", after(a_x3, other_2))

    a_parts = [a, a_1, a_2, a_3, a_x, a_x1, a_x2, a_x3]
    a_parts += [other, other_1, other_2, other_3, other_x, other_x1, other_x2, other_x3]
    b_parts = [b, b_1, b_2, b_3, b_x, b_x1, b_x2, b_x3]
    return multiply(a_parts, b_parts, a_where, b_where, b_row)


def solution(mesh):
    in_specs = (P(None, None, "rcv", "shot"), P(None, None, "shot", "rcv"), P())
    out_specs = P(None, None, "shot", "rcv")
    return jax.shard_map(
        per_device, mesh=mesh, in_specs=in_specs, out_specs=out_specs, check_vma=False
    )
```

```python
import functools

import jax
import jax.numpy as jnp
from jax import lax
from jax.experimental import pallas as pl
from jax.experimental.pallas import tpu as pltpu
from jax.sharding import PartitionSpec as P

BLK = 32
STEPS = 12
ROWS = 256
AXES = ("shot", "rcv")
X, Y, Z, CORES = 4, 4, 4, 2


def moved(value, dx=0, dy=0, dz=0, flip_x=False, flip_core=False):
    def index(x, y, z, core):
        x_hi, x_lo = divmod(x, 2)
        return (((x_hi * Y + y) * 2 + x_lo) * Z + z) * CORES + core

    pairs = []
    for x in range(X):
        for y in range(Y):
            for z in range(Z):
                for core in range(CORES):
                    way = 1 - 2 * core
                    to_x = x ^ 1 if flip_x else (x + way * dx) % X
                    to_core = core ^ 1 if flip_core else core
                    target = index(to_x, (y + way * dy) % Y, (z + way * dz) % Z, to_core)
                    pairs.append((index(x, y, z, core), target))
    return lax.ppermute(value, AXES, pairs)


def choose(refs, which, act):
    if len(refs) == 1:
        act(refs[0])
        return
    half = len(refs) // 2

    @pl.when(which < half)
    def _():
        choose(refs[:half], which, act)

    @pl.when(which >= half)
    def _():
        choose(refs[half:], which - half, act)


def multiply_kernel(carried_by_other, ids, place, *refs):
    a_refs, b_refs = refs[:8], refs[8:16]
    out, a_buf, b_buf, lhs, rhs, a_sem, b_sem = refs[-7:]
    f = pl.program_id(0)
    rcvs = b_buf.shape[4]
    shot, rcv = place[0], place[1]
    core, z, x_lo = rcv % CORES, rcv // CORES % Z, rcv // (CORES * Z)
    y, x_hi = shot % Y, shot // Y
    carrier = core ^ carried_by_other

    def fetch(freq):
        for step in range(STEPS):
            block = ids[step]
            of_core, of_z, of_x = block % CORES, block // CORES % Z, block // (CORES * Z)
            distance = jnp.where(carrier == 0, z - of_z, of_z - z) & (Z - 1)
            slot = of_core ^ carrier

            def from_surface(ref):
                pltpu.make_async_copy(
                    ref.at[slot, freq], a_buf.at[freq, step], a_sem.at[freq]
                ).start()

            choose(a_refs, (of_x ^ x_lo) * Z + distance, from_surface)

            owner = block // 2
            distance = jnp.where(core == 0, y - owner % Y, owner % Y - y) & (Y - 1)
            rows = pl.ds(pl.multiple_of(block % 2 * BLK, BLK), BLK)

            def from_traces(ref):
                pltpu.make_async_copy(
                    ref.at[2 * carrier + freq, :, rows], b_buf.at[freq, step], b_sem.at[freq]
                ).start()

            choose(b_refs, (owner // Y ^ x_hi) * Y + distance, from_traces)

    @pl.when(f == 0)
    def _():
        for freq in range(a_buf.shape[0]):
            fetch(freq)

    for buf, sem in ((a_buf, a_sem), (b_buf, b_sem)):
        pltpu.make_async_copy(buf.at[f], buf.at[f], sem.at[f]).wait()

    for step in range(STEPS):
        real = b_buf[f, step, 0]
        imag = b_buf[f, step, 1]
        rhs[0, step, 0] = real
        rhs[0, step, 1] = -imag
        rhs[1, step, 0] = imag
        rhs[1, step, 1] = real

    depth = STEPS * 2 * BLK
    for first in range(0, lhs.shape[0], ROWS):
        block = a_buf[f, :, :, :, first : first + ROWS].reshape(depth, ROWS)
        lhs[first : first + ROWS, :] = block.T

    for part in range(2):
        out[0, part] = jnp.dot(
            lhs[...], rhs[part].reshape(depth, rcvs), preferred_element_type=jnp.float32
        ).astype(out.dtype)


def multiply(a_parts, b_parts, block_ids, place, done=None):
    _, count, _, _, shots = a_parts[0].shape
    freqs, _, _, rcvs = b_parts[0].shape
    depth = STEPS * 2 * BLK
    by_other = int(done is not None)
    operands = [block_ids, place, *a_parts, *b_parts] + ([done] if by_other else [])
    return pl.pallas_call(
        functools.partial(multiply_kernel, by_other),
        out_shape=jax.ShapeDtypeStruct((freqs, 2, shots, rcvs), jnp.bfloat16),
        grid_spec=pltpu.PrefetchScalarGridSpec(
            num_scalar_prefetch=2,
            grid=(count,),
            in_specs=[pl.BlockSpec(memory_space=pl.ANY)] * (len(operands) - 2),
            out_specs=pl.BlockSpec(
                (1, 2, shots, rcvs),
                lambda f, ids, place: (2 * (place[1] % CORES ^ by_other) + f, 0, 0, 0),
            ),
            scratch_shapes=[
                pltpu.VMEM((count, STEPS, 2, BLK, shots), jnp.bfloat16),
                pltpu.VMEM((count, STEPS, 2, BLK, rcvs), jnp.bfloat16),
                pltpu.VMEM((shots, depth), jnp.bfloat16),
                pltpu.VMEM((2, STEPS, 2, BLK, rcvs), jnp.bfloat16),
                pltpu.SemaphoreType.DMA((count,)),
                pltpu.SemaphoreType.DMA((count,)),
            ],
        ),
        input_output_aliases={len(operands) - 1: 0} if by_other else {},
        compiler_params=pltpu.CompilerParams(vmem_limit_bytes=56 * 1024 * 1024),
        cost_estimate=pl.CostEstimate(
            flops=2 * count * shots * 2 * rcvs * depth,
            bytes_accessed=10 * 1024 * 1024,
            transcendentals=0,
        ),
    )(*operands)


def after(value, *earlier):
    return lax.optimization_barrier((value, *earlier))[0]


def per_device(surface_data, source_traces, block_ids):
    a, b = surface_data, source_traces
    core = lax.axis_index("rcv") % CORES
    place = jnp.stack([lax.axis_index("shot"), lax.axis_index("rcv")]).astype(jnp.int32)

    def send(name, value, **way):
        with jax.named_scope(name):
            return moved(value, **way)

    def swap(name, value):
        return send(name, value, flip_core=True)

    other = swap("other", a)
    own = jnp.where(core == 0, jnp.stack([a[:2], other[:2]]), jnp.stack([a[2:], other[2:]]))
    b_1 = send("b_1", b, dy=1)
    b_x = send("b_x", b, dx=2)
    a_1 = send("a_1", own, dz=1)
    b_3 = send("b_3", after(b, other), dy=-1)
    a_3 = send("a_3", after(own, other, place), dz=-1)
    b_2 = send("b_2", b_1, dy=1)
    a_x = send("a_x", after(own, b_x), flip_x=True)
    a_2 = send("a_2", a_1, dz=1)
    b_x1 = send("b_x1", after(b_x, b_3), dy=1)
    b_x3 = send("b_x3", after(b_x, a_3), dy=-1)
    their = swap("their", after(own, b_2))
    a_x1 = send("a_x1", after(a_x, a_2), dz=1)
    a_x2 = send("a_x2", a_2, flip_x=True)
    a_x3 = send("a_x3", after(a_x, b_x1), dz=-1)
    b_x2 = send("b_x2", after(b_x1, b_x3), dy=1)
    their_x = swap("their_x", after(a_x, their))
    their_3 = swap("their_3", after(a_3, a_x1))
    their_2 = swap("their_2", after(a_2, a_x2))
    their_1 = swap("their_1", after(a_1, a_x3))
    their_x3 = swap("their_x3", after(a_x3, b_x2))
    their_x1 = swap("their_x1", after(a_x1, their_x))
    their_x2 = swap("their_x2", after(a_x2, their_3))

    b_parts = [b, b_1, b_2, b_3, b_x, b_x1, b_x2, b_x3]
    a_parts = [own, a_1, a_2, a_3, a_x, a_x1, a_x2, a_x3]
    result = multiply(a_parts, b_parts, block_ids, place)
    a_parts = [their, their_1, their_2, their_3, their_x, their_x1, their_x2, their_x3]
    return multiply(a_parts, b_parts, block_ids, place, result)


def solution(mesh):
    in_specs = (P(None, None, "rcv", "shot"), P(None, None, "shot", "rcv"), P())
    out_specs = P(None, None, "shot", "rcv")
    return jax.shard_map(
        per_device, mesh=mesh, in_specs=in_specs, out_specs=out_specs, check_vma=False
    )
```

```python
import jax
import jax.numpy as jnp
from jax import lax
from jax.experimental import pallas as pl
from jax.experimental.pallas import tpu as pltpu
from jax.sharding import PartitionSpec as P

BLK = 32
STEPS = 12
ROWS = 256
SURFACE_ORDER = (3, 4, 5, 6, 7, 8, 9, 10, 11, 12, 13, 14, 1, 2, 15, 0)
AXES = ("shot", "rcv")
X, Y, Z, CORES = 4, 4, 4, 2


def moved(value, dx=0, dy=0, dz=0, flip_x=False, flip_core=False):
    def index(x, y, z, core):
        x_hi, x_lo = divmod(x, 2)
        return (((x_hi * Y + y) * 2 + x_lo) * Z + z) * CORES + core

    pairs = []
    for x in range(X):
        for y in range(Y):
            for z in range(Z):
                for core in range(CORES):
                    way = 1 - 2 * core
                    to_x = x ^ 1 if flip_x else (x + way * dx) % X
                    to_core = core ^ 1 if flip_core else core
                    target = index(to_x, (y + way * dy) % Y, (z + way * dz) % Z, to_core)
                    pairs.append((index(x, y, z, core), target))
    return lax.ppermute(value, AXES, pairs)


def choose(refs, which, act):
    if len(refs) == 1:
        act(refs[0])
        return
    half = len(refs) // 2

    @pl.when(which < half)
    def _():
        choose(refs[:half], which, act)

    @pl.when(which >= half)
    def _():
        choose(refs[half:], which - half, act)


def multiply_kernel(a_where, b_where, b_row, *refs):
    a_refs, b_refs = [refs[i] for i in SURFACE_ORDER], refs[16:24]
    out, a_buf, b_buf, lhs, rhs, a_sem, b_sem = refs[24:]
    freqs = a_buf.shape[1]
    f = pl.program_id(0)
    rcvs = b_buf.shape[4]

    def fetch(first_freq, count, slot):
        these = pl.ds(first_freq, count)
        for step in range(STEPS):

            def from_surface(ref):
                pltpu.make_async_copy(
                    ref.at[these], a_buf.at[step, these], a_sem.at[slot]
                ).start()

            choose(a_refs, a_where[step], from_surface)

            def from_traces(ref):
                first = pl.multiple_of(b_row[step], BLK)
                pltpu.make_async_copy(
                    ref.at[these, :, pl.ds(first, BLK)], b_buf.at[step, these], b_sem.at[slot]
                ).start()

            choose(b_refs, b_where[step], from_traces)

    def arrive(first_freq, count, slot):
        these = pl.ds(first_freq, count)
        for buf, sem in ((a_buf, a_sem), (b_buf, b_sem)):
            part = buf.at[:, these]
            pltpu.make_async_copy(part, part, sem.at[slot]).wait()

    @pl.when(f == 0)
    def _():
        fetch(0, 1, 0)
        fetch(1, freqs - 1, 1)
        arrive(0, 1, 0)

    @pl.when(f == 1)
    def _():
        arrive(1, freqs - 1, 1)

    for step in range(STEPS):
        real = b_buf[step, f, 0]
        imag = b_buf[step, f, 1]
        rhs[step, 0, :, :rcvs] = real
        rhs[step, 0, :, rcvs:] = imag
        rhs[step, 1, :, :rcvs] = -imag
        rhs[step, 1, :, rcvs:] = real

    depth = STEPS * 2 * BLK
    for first in range(0, lhs.shape[0], ROWS):
        block = a_buf[:, f, :, :, first : first + ROWS].reshape(depth, ROWS)
        lhs[first : first + ROWS, :] = block.T

    product = jnp.dot(
        lhs[...], rhs[...].reshape(depth, 2 * rcvs), preferred_element_type=jnp.float32
    ).astype(out.dtype)
    out[0, 0] = product[:, :rcvs]
    out[0, 1] = product[:, rcvs:]


def multiply(a_parts, b_parts, a_where, b_where, b_row):
    freqs, _, _, shots = a_parts[0].shape
    rcvs = b_parts[0].shape[3]
    depth = STEPS * 2 * BLK
    return pl.pallas_call(
        multiply_kernel,
        out_shape=jax.ShapeDtypeStruct((freqs, 2, shots, rcvs), jnp.bfloat16),
        grid_spec=pltpu.PrefetchScalarGridSpec(
            num_scalar_prefetch=3,
            grid=(freqs,),
            in_specs=[pl.BlockSpec(memory_space=pl.ANY)] * (len(a_parts) + len(b_parts)),
            out_specs=pl.BlockSpec((1, 2, shots, rcvs), lambda f, *_: (f, 0, 0, 0)),
            scratch_shapes=[
                pltpu.VMEM((STEPS, freqs, 2, BLK, shots), jnp.bfloat16),
                pltpu.VMEM((STEPS, freqs, 2, BLK, rcvs), jnp.bfloat16),
                pltpu.VMEM((shots, depth), jnp.bfloat16),
                pltpu.VMEM((STEPS, 2, BLK, 2 * rcvs), jnp.bfloat16),
                pltpu.SemaphoreType.DMA((2,)),
                pltpu.SemaphoreType.DMA((2,)),
            ],
        ),
        compiler_params=pltpu.CompilerParams(vmem_limit_bytes=52 * 1024 * 1024),
        cost_estimate=pl.CostEstimate(
            flops=2 * freqs * shots * 2 * rcvs * depth,
            bytes_accessed=20 * 1024 * 1024,
            transcendentals=0,
        ),
    )(a_where, b_where, b_row, *a_parts, *b_parts)


def places(block_ids):
    shot, rcv = lax.axis_index("shot"), lax.axis_index("rcv")
    core, z, x_lo = rcv % CORES, rcv // CORES % Z, rcv // (CORES * Z)
    of_core, of_z, of_x = block_ids % CORES, block_ids // CORES % Z, block_ids // (CORES * Z)
    distance = jnp.where(of_core == 0, z - of_z, of_z - z) % Z
    a_where = ((of_core != core) * 2 + (of_x != x_lo)) * Z + distance
    owner = block_ids // 2
    y, of_y = shot % Y, owner % Y
    distance = jnp.where(core == 0, y - of_y, of_y - y) % Y
    b_where = (shot // Y != owner // Y) * Y + distance
    return a_where.astype(jnp.int32), b_where.astype(jnp.int32), block_ids % 2 * BLK


def after(value, *earlier):
    return lax.optimization_barrier((value, *earlier))[0]


def per_device(surface_data, source_traces, block_ids):
    a, b = surface_data, source_traces
    a_where, b_where, b_row = places(block_ids)

    def send(name, value, **way):
        with jax.named_scope(name):
            return moved(value, **way)

    def swap(name, value):
        return send(name, value, flip_core=True)

    b_3 = send("b_3", b, dy=-1)
    b_x = send("b_x", b, dx=2)
    a_3 = send("a_3", a, dz=-1)
    b_1 = send("b_1", b, dy=1)
    a_1 = send("a_1", a, dz=1)
    a_x = send("a_x", after(a, b_3, a_where, b_where, b_row), flip_x=True)
    other_3 = swap("other_3", after(a_3, b_x))
    b_x1 = send("b_x1", after(b_x, a_3), dy=1)
    a_2 = send("a_2", after(a_1, b_1), dz=1)
    b_x3 = send("b_x3", after(b_x, a_1), dy=-1)
    a_x3 = send("a_x3", a_x, dz=-1)
    b_2 = send("b_2", after(b_1, other_3), dy=1)
    a_x2 = send("a_x2", after(a_2, b_x1), flip_x=True)
    b_x2 = send("b_x2", after(b_x1, a_2), dy=1)
    a_x1 = send("a_x1", after(a_x, b_x3), dz=1)
    other = swap("other", after(a, a_x3))
    other_2 = swap("other_2", after(a_2, b_2))
    other_1 = swap("other_1", after(a_1, a_x2))
    other_x2 = swap("other_x2", after(a_x2, b_x2))
    other_x1 = swap("other_x1", a_x1)
    other_x = swap("other_x", after(a_x, other))
    other_x3 = swap("other_x3", after(a_x3, other_2))

    a_parts = [other_x3, other_x, other_x1, a, a_1, a_2, a_3, a_x]
    a_parts += [a_x1, a_x2, a_x3, other, other_1, other_2, other_3, other_x2]
    b_parts = [b, b_1, b_2, b_3, b_x, b_x1, b_x2, b_x3]
    return multiply(a_parts, b_parts, a_where, b_where, b_row)


def solution(mesh):
    in_specs = (P(None, None, "rcv", "shot"), P(None, None, "shot", "rcv"), P())
    out_specs = P(None, None, "shot", "rcv")
    return jax.shard_map(
        per_device, mesh=mesh, in_specs=in_specs, out_specs=out_specs, check_vma=False
    )
```

```python
import jax
import jax.numpy as jnp
from jax import lax
from jax.experimental import pallas as pl
from jax.experimental.pallas import tpu as pltpu
from jax.sharding import PartitionSpec as P

BLK = 32
STEPS = 12
ROWS = 256
AXES = ("shot", "rcv")
X, Y, Z, CORES = 4, 4, 4, 2


def moved(value, dx=0, dy=0, dz=0, flip_x=False, flip_core=False):
    def index(x, y, z, core):
        x_hi, x_lo = divmod(x, 2)
        return (((x_hi * Y + y) * 2 + x_lo) * Z + z) * CORES + core

    pairs = []
    for x in range(X):
        for y in range(Y):
            for z in range(Z):
                for core in range(CORES):
                    way = 1 - 2 * core
                    to_x = x ^ 1 if flip_x else (x + way * dx) % X
                    to_core = core ^ 1 if flip_core else core
                    target = index(to_x, (y + way * dy) % Y, (z + way * dz) % Z, to_core)
                    pairs.append((index(x, y, z, core), target))
    return lax.ppermute(value, AXES, pairs)


def choose(refs, which, act):
    if len(refs) == 1:
        act(refs[0])
        return
    half = len(refs) // 2

    @pl.when(which < half)
    def _():
        choose(refs[:half], which, act)

    @pl.when(which >= half)
    def _():
        choose(refs[half:], which - half, act)


def multiply_kernel(a_where, b_where, b_row, *refs):
    a_refs, b_refs = refs[:16], refs[16:24]
    out, a_buf, b_buf, lhs, rhs, a_sem, b_sem = refs[24:]
    freqs = a_buf.shape[1]
    f = pl.program_id(0)
    rcvs = b_buf.shape[4]

    def fetch(first_freq, count, slot):
        these = pl.ds(first_freq, count)
        for step in range(STEPS):

            def from_surface(ref):
                pltpu.make_async_copy(
                    ref.at[these], a_buf.at[step, these], a_sem.at[slot]
                ).start()

            choose(a_refs, a_where[step], from_surface)

            def from_traces(ref):
                first = pl.multiple_of(b_row[step], BLK)
                pltpu.make_async_copy(
                    ref.at[these, :, pl.ds(first, BLK)], b_buf.at[step, these], b_sem.at[slot]
                ).start()

            choose(b_refs, b_where[step], from_traces)

    def arrive(first_freq, count, slot):
        these = pl.ds(first_freq, count)
        for buf, sem in ((a_buf, a_sem), (b_buf, b_sem)):
            part = buf.at[:, these]
            pltpu.make_async_copy(part, part, sem.at[slot]).wait()

    @pl.when(f == 0)
    def _():
        fetch(0, 1, 0)
        fetch(1, freqs - 1, 1)
        arrive(0, 1, 0)

    @pl.when(f == 1)
    def _():
        arrive(1, freqs - 1, 1)

    for step in range(STEPS):
        real = b_buf[step, f, 0]
        imag = b_buf[step, f, 1]
        rhs[step, 0, :, :rcvs] = real
        rhs[step, 0, :, rcvs:] = imag
        rhs[step, 1, :, :rcvs] = -imag
        rhs[step, 1, :, rcvs:] = real

    depth = STEPS * 2 * BLK
    for first in range(0, lhs.shape[0], ROWS):
        block = a_buf[:, f, :, :, first : first + ROWS].reshape(depth, ROWS)
        lhs[first : first + ROWS, :] = block.T

    product = jnp.dot(
        lhs[...], rhs[...].reshape(depth, 2 * rcvs), preferred_element_type=jnp.float32
    ).astype(out.dtype)
    out[0, 0] = product[:, :rcvs]
    out[0, 1] = product[:, rcvs:]


def multiply(a_parts, b_parts, a_where, b_where, b_row):
    freqs, _, _, shots = a_parts[0].shape
    rcvs = b_parts[0].shape[3]
    depth = STEPS * 2 * BLK
    return pl.pallas_call(
        multiply_kernel,
        out_shape=jax.ShapeDtypeStruct((freqs, 2, shots, rcvs), jnp.bfloat16),
        grid_spec=pltpu.PrefetchScalarGridSpec(
            num_scalar_prefetch=3,
            grid=(freqs,),
            in_specs=[pl.BlockSpec(memory_space=pl.ANY)] * (len(a_parts) + len(b_parts)),
            out_specs=pl.BlockSpec((1, 2, shots, rcvs), lambda f, *_: (f, 0, 0, 0)),
            scratch_shapes=[
                pltpu.VMEM((STEPS, freqs, 2, BLK, shots), jnp.bfloat16),
                pltpu.VMEM((STEPS, freqs, 2, BLK, rcvs), jnp.bfloat16),
                pltpu.VMEM((shots, depth), jnp.bfloat16),
                pltpu.VMEM((STEPS, 2, BLK, 2 * rcvs), jnp.bfloat16),
                pltpu.SemaphoreType.DMA((2,)),
                pltpu.SemaphoreType.DMA((2,)),
            ],
        ),
        compiler_params=pltpu.CompilerParams(vmem_limit_bytes=56 * 1024 * 1024),
        cost_estimate=pl.CostEstimate(
            flops=2 * freqs * shots * 2 * rcvs * depth,
            bytes_accessed=20 * 1024 * 1024,
            transcendentals=0,
        ),
    )(a_where, b_where, b_row, *a_parts, *b_parts)


def places(block_ids):
    shot, rcv = lax.axis_index("shot"), lax.axis_index("rcv")
    core, z, x_lo = rcv % CORES, rcv // CORES % Z, rcv // (CORES * Z)
    of_core, of_z, of_x = block_ids % CORES, block_ids // CORES % Z, block_ids // (CORES * Z)
    distance = jnp.where(of_core == 0, z - of_z, of_z - z) % Z
    a_where = ((of_core != core) * 2 + (of_x != x_lo)) * Z + distance
    owner = block_ids // 2
    y, of_y = shot % Y, owner % Y
    distance = jnp.where(core == 0, y - of_y, of_y - y) % Y
    b_where = (shot // Y != owner // Y) * Y + distance
    return a_where.astype(jnp.int32), b_where.astype(jnp.int32), block_ids % 2 * BLK


def after(value, *earlier):
    return lax.optimization_barrier((value, *earlier))[0]


def per_device(surface_data, source_traces, block_ids):
    a, b = surface_data, source_traces
    a_where, b_where, b_row = places(block_ids)

    def send(name, value, **way):
        with jax.named_scope(name):
            return moved(value, **way)

    def swap(name, value):
        return send(name, value, flip_core=True)

    b_3 = send("b_3", b, dy=-1)
    b_x = send("b_x", b, dx=2)
    a_3 = send("a_3", a, dz=-1)
    b_1 = send("b_1", b, dy=1)
    a_1 = send("a_1", a, dz=1)
    a_x = send("a_x", after(a, b_3, a_where, b_where, b_row), flip_x=True)
    other_3 = swap("other_3", after(a_3, b_x))
    b_x1 = send("b_x1", after(b_x, a_3), dy=1)
    a_2 = send("a_2", after(a_1, b_1), dz=1)
    b_x3 = send("b_x3", after(b_x, a_1), dy=-1)
    b_2 = send("b_2", after(b_1, a_x), dy=1)
    a_x3 = send("a_x3", after(a_x, other_3), dz=-1)
    a_x2 = send("a_x2", after(a_2, b_x1), flip_x=True)
    b_x2 = send("b_x2", after(b_x1, a_2), dy=1)
    a_x1 = send("a_x1", after(a_x, b_x3), dz=1)
    other_2 = swap("other_2", after(a_2, b_2))
    other_1 = swap("other_1", after(a_1, a_x3))
    other_x2 = swap("other_x2", a_x2)
    other = swap("other", after(a, b_x2))
    other_x1 = swap("other_x1", a_x1)
    other_x3 = swap("other_x3", after(a_x3, other_2))
    other_x = swap("other_x", after(a_x, other_1))

    a_parts = [a, a_1, a_2, a_3, a_x, a_x1, a_x2, a_x3]
    a_parts += [other, other_1, other_2, other_3, other_x, other_x1, other_x2, other_x3]
    b_parts = [b, b_1, b_2, b_3, b_x, b_x1, b_x2, b_x3]
    return multiply(a_parts, b_parts, a_where, b_where, b_row)


def solution(mesh):
    in_specs = (P(None, None, "rcv", "shot"), P(None, None, "shot", "rcv"), P())
    out_specs = P(None, None, "shot", "rcv")
    return jax.shard_map(
        per_device, mesh=mesh, in_specs=in_specs, out_specs=out_specs, check_vma=False
    )
```

```python
import jax
import jax.numpy as jnp
from jax import lax
from jax.experimental import pallas as pl
from jax.experimental.pallas import tpu as pltpu
from jax.sharding import PartitionSpec as P

BLK = 32
STEPS = 12
ROWS = 256
SURFACE_ORDER = (1, 2, 3, 4, 5, 6, 7, 8, 9, 10, 11, 12, 13, 14, 15, 0)
AXES = ("shot", "rcv")
X, Y, Z, CORES = 4, 4, 4, 2


def moved(value, dx=0, dy=0, dz=0, flip_x=False, flip_core=False):
    def index(x, y, z, core):
        x_hi, x_lo = divmod(x, 2)
        return (((x_hi * Y + y) * 2 + x_lo) * Z + z) * CORES + core

    pairs = []
    for x in range(X):
        for y in range(Y):
            for z in range(Z):
                for core in range(CORES):
                    way = 1 - 2 * core
                    to_x = x ^ 1 if flip_x else (x + way * dx) % X
                    to_core = core ^ 1 if flip_core else core
                    target = index(to_x, (y + way * dy) % Y, (z + way * dz) % Z, to_core)
                    pairs.append((index(x, y, z, core), target))
    return lax.ppermute(value, AXES, pairs)


def choose(refs, which, act):
    if len(refs) == 1:
        act(refs[0])
        return
    half = len(refs) // 2

    @pl.when(which < half)
    def _():
        choose(refs[:half], which, act)

    @pl.when(which >= half)
    def _():
        choose(refs[half:], which - half, act)


def multiply_kernel(a_where, b_where, b_row, *refs):
    a_refs, b_refs = [refs[i] for i in SURFACE_ORDER], refs[16:24]
    out, a_buf, b_buf, lhs, rhs, a_sem, b_sem = refs[24:]
    freqs = a_buf.shape[1]
    f = pl.program_id(0)
    rcvs = b_buf.shape[4]

    def fetch(first_freq, count, slot):
        these = pl.ds(first_freq, count)
        for step in range(STEPS):

            def from_surface(ref):
                pltpu.make_async_copy(
                    ref.at[these], a_buf.at[step, these], a_sem.at[slot]
                ).start()

            choose(a_refs, a_where[step], from_surface)

            def from_traces(ref):
                first = pl.multiple_of(b_row[step], BLK)
                pltpu.make_async_copy(
                    ref.at[these, :, pl.ds(first, BLK)], b_buf.at[step, these], b_sem.at[slot]
                ).start()

            choose(b_refs, b_where[step], from_traces)

    def arrive(first_freq, count, slot):
        these = pl.ds(first_freq, count)
        for buf, sem in ((a_buf, a_sem), (b_buf, b_sem)):
            part = buf.at[:, these]
            pltpu.make_async_copy(part, part, sem.at[slot]).wait()

    @pl.when(f == 0)
    def _():
        fetch(0, 1, 0)
        fetch(1, freqs - 1, 1)
        arrive(0, 1, 0)

    @pl.when(f == 1)
    def _():
        arrive(1, freqs - 1, 1)

    for step in range(STEPS):
        real = b_buf[step, f, 0]
        imag = b_buf[step, f, 1]
        rhs[step, 0, :, :rcvs] = real
        rhs[step, 0, :, rcvs:] = imag
        rhs[step, 1, :, :rcvs] = -imag
        rhs[step, 1, :, rcvs:] = real

    depth = STEPS * 2 * BLK
    for first in range(0, lhs.shape[0], ROWS):
        block = a_buf[:, f, :, :, first : first + ROWS].reshape(depth, ROWS)
        lhs[first : first + ROWS, :] = block.T

    product = jnp.dot(
        lhs[...], rhs[...].reshape(depth, 2 * rcvs), preferred_element_type=jnp.float32
    ).astype(out.dtype)
    out[0, 0] = product[:, :rcvs]
    out[0, 1] = product[:, rcvs:]


def multiply(a_parts, b_parts, a_where, b_where, b_row):
    freqs, _, _, shots = a_parts[0].shape
    rcvs = b_parts[0].shape[3]
    depth = STEPS * 2 * BLK
    return pl.pallas_call(
        multiply_kernel,
        out_shape=jax.ShapeDtypeStruct((freqs, 2, shots, rcvs), jnp.bfloat16),
        grid_spec=pltpu.PrefetchScalarGridSpec(
            num_scalar_prefetch=3,
            grid=(freqs,),
            in_specs=[pl.BlockSpec(memory_space=pl.ANY)] * (len(a_parts) + len(b_parts)),
            out_specs=pl.BlockSpec((1, 2, shots, rcvs), lambda f, *_: (f, 0, 0, 0)),
            scratch_shapes=[
                pltpu.VMEM((STEPS, freqs, 2, BLK, shots), jnp.bfloat16),
                pltpu.VMEM((STEPS, freqs, 2, BLK, rcvs), jnp.bfloat16),
                pltpu.VMEM((shots, depth), jnp.bfloat16),
                pltpu.VMEM((STEPS, 2, BLK, 2 * rcvs), jnp.bfloat16),
                pltpu.SemaphoreType.DMA((2,)),
                pltpu.SemaphoreType.DMA((2,)),
            ],
        ),
        compiler_params=pltpu.CompilerParams(vmem_limit_bytes=53 * 1024 * 1024),
        cost_estimate=pl.CostEstimate(
            flops=2 * freqs * shots * 2 * rcvs * depth,
            bytes_accessed=20 * 1024 * 1024,
            transcendentals=0,
        ),
    )(a_where, b_where, b_row, *a_parts, *b_parts)


def places(block_ids):
    shot, rcv = lax.axis_index("shot"), lax.axis_index("rcv")
    core, z, x_lo = rcv % CORES, rcv // CORES % Z, rcv // (CORES * Z)
    of_core, of_z, of_x = block_ids % CORES, block_ids // CORES % Z, block_ids // (CORES * Z)
    distance = jnp.where(of_core == 0, z - of_z, of_z - z) % Z
    a_where = ((of_core != core) * 2 + (of_x != x_lo)) * Z + distance
    owner = block_ids // 2
    y, of_y = shot % Y, owner % Y
    distance = jnp.where(core == 0, y - of_y, of_y - y) % Y
    b_where = (shot // Y != owner // Y) * Y + distance
    return a_where.astype(jnp.int32), b_where.astype(jnp.int32), block_ids % 2 * BLK


def after(value, *earlier):
    return lax.optimization_barrier((value, *earlier))[0]


def per_device(surface_data, source_traces, block_ids):
    a, b = surface_data, source_traces
    a_where, b_where, b_row = places(block_ids)

    def send(name, value, **way):
        with jax.named_scope(name):
            return moved(value, **way)

    def swap(name, value):
        return send(name, value, flip_core=True)

    b_3 = send("b_3", b, dy=-1)
    b_x = send("b_x", b, dx=2)
    a_3 = send("a_3", a, dz=-1)
    b_1 = send("b_1", b, dy=1)
    a_1 = send("a_1", a, dz=1)
    a_x = send("a_x", after(a, b_3, a_where, b_where, b_row), flip_x=True)
    other_3 = swap("other_3", after(a_3, b_x))
    b_x1 = send("b_x1", after(b_x, a_3), dy=1)
    a_2 = send("a_2", after(a_1, b_1), dz=1)
    b_x3 = send("b_x3", after(b_x, a_1), dy=-1)
    a_x3 = send("a_x3", a_x, dz=-1)
    b_2 = send("b_2", after(b_1, other_3), dy=1)
    a_x2 = send("a_x2", after(a_2, b_x1), flip_x=True)
    b_x2 = send("b_x2", after(b_x1, a_2), dy=1)
    a_x1 = send("a_x1", after(a_x, b_x3), dz=1)
    other = swap("other", after(a, a_x3))
    other_2 = swap("other_2", after(a_2, b_2))
    other_1 = swap("other_1", after(a_1, a_x2))
    other_x2 = swap("other_x2", after(a_x2, b_x2))
    other_x1 = swap("other_x1", a_x1)
    other_x = swap("other_x", after(a_x, other))
    other_x3 = swap("other_x3", after(a_x3, other_2))

    a_parts = [other_x3, a, a_1, a_2, a_3, a_x, a_x1, a_x2]
    a_parts += [a_x3, other, other_1, other_2, other_3, other_x, other_x1, other_x2]
    b_parts = [b, b_1, b_2, b_3, b_x, b_x1, b_x2, b_x3]
    return multiply(a_parts, b_parts, a_where, b_where, b_row)


def solution(mesh):
    in_specs = (P(None, None, "rcv", "shot"), P(None, None, "shot", "rcv"), P())
    out_specs = P(None, None, "shot", "rcv")
    return jax.shard_map(
        per_device, mesh=mesh, in_specs=in_specs, out_specs=out_specs, check_vma=False
    )
```

```python
import jax
import jax.numpy as jnp
from jax import lax
from jax.experimental import pallas as pl
from jax.experimental.pallas import tpu as pltpu
from jax.sharding import PartitionSpec as P

BLK = 32
STEPS = 12
ROWS = 256
SURFACE_ORDER = (2, 3, 4, 5, 6, 7, 8, 9, 10, 11, 12, 13, 1, 14, 15, 0)
AXES = ("shot", "rcv")
X, Y, Z, CORES = 4, 4, 4, 2


def moved(value, dx=0, dy=0, dz=0, flip_x=False, flip_core=False):
    def index(x, y, z, core):
        x_hi, x_lo = divmod(x, 2)
        return (((x_hi * Y + y) * 2 + x_lo) * Z + z) * CORES + core

    pairs = []
    for x in range(X):
        for y in range(Y):
            for z in range(Z):
                for core in range(CORES):
                    way = 1 - 2 * core
                    to_x = x ^ 1 if flip_x else (x + way * dx) % X
                    to_core = core ^ 1 if flip_core else core
                    target = index(to_x, (y + way * dy) % Y, (z + way * dz) % Z, to_core)
                    pairs.append((index(x, y, z, core), target))
    return lax.ppermute(value, AXES, pairs)


def choose(refs, which, act):
    if len(refs) == 1:
        act(refs[0])
        return
    half = len(refs) // 2

    @pl.when(which < half)
    def _():
        choose(refs[:half], which, act)

    @pl.when(which >= half)
    def _():
        choose(refs[half:], which - half, act)


def multiply_kernel(a_where, b_where, b_row, *refs):
    a_refs, b_refs = [refs[i] for i in SURFACE_ORDER], refs[16:24]
    out, a_buf, b_buf, lhs, rhs, a_sem, b_sem = refs[24:]
    freqs = a_buf.shape[1]
    f = pl.program_id(0)
    rcvs = b_buf.shape[4]

    def fetch(first_freq, count, slot):
        these = pl.ds(first_freq, count)
        for step in range(STEPS):

            def from_surface(ref):
                pltpu.make_async_copy(
                    ref.at[these], a_buf.at[step, these], a_sem.at[slot]
                ).start()

            choose(a_refs, a_where[step], from_surface)

            def from_traces(ref):
                first = pl.multiple_of(b_row[step], BLK)
                pltpu.make_async_copy(
                    ref.at[these, :, pl.ds(first, BLK)], b_buf.at[step, these], b_sem.at[slot]
                ).start()

            choose(b_refs, b_where[step], from_traces)

    def arrive(first_freq, count, slot):
        these = pl.ds(first_freq, count)
        for buf, sem in ((a_buf, a_sem), (b_buf, b_sem)):
            part = buf.at[:, these]
            pltpu.make_async_copy(part, part, sem.at[slot]).wait()

    @pl.when(f == 0)
    def _():
        fetch(0, 1, 0)
        fetch(1, freqs - 1, 1)
        arrive(0, 1, 0)

    @pl.when(f == 1)
    def _():
        arrive(1, freqs - 1, 1)

    for step in range(STEPS):
        real = b_buf[step, f, 0]
        imag = b_buf[step, f, 1]
        rhs[step, 0, :, :rcvs] = real
        rhs[step, 0, :, rcvs:] = imag
        rhs[step, 1, :, :rcvs] = -imag
        rhs[step, 1, :, rcvs:] = real

    depth = STEPS * 2 * BLK
    for first in range(0, lhs.shape[0], ROWS):
        block = a_buf[:, f, :, :, first : first + ROWS].reshape(depth, ROWS)
        lhs[first : first + ROWS, :] = block.T

    product = jnp.dot(
        lhs[...], rhs[...].reshape(depth, 2 * rcvs), preferred_element_type=jnp.float32
    ).astype(out.dtype)
    out[0, 0] = product[:, :rcvs]
    out[0, 1] = product[:, rcvs:]


def multiply(a_parts, b_parts, a_where, b_where, b_row):
    freqs, _, _, shots = a_parts[0].shape
    rcvs = b_parts[0].shape[3]
    depth = STEPS * 2 * BLK
    return pl.pallas_call(
        multiply_kernel,
        out_shape=jax.ShapeDtypeStruct((freqs, 2, shots, rcvs), jnp.bfloat16),
        grid_spec=pltpu.PrefetchScalarGridSpec(
            num_scalar_prefetch=3,
            grid=(freqs,),
            in_specs=[pl.BlockSpec(memory_space=pl.ANY)] * (len(a_parts) + len(b_parts)),
            out_specs=pl.BlockSpec((1, 2, shots, rcvs), lambda f, *_: (f, 0, 0, 0)),
            scratch_shapes=[
                pltpu.VMEM((STEPS, freqs, 2, BLK, shots), jnp.bfloat16),
                pltpu.VMEM((STEPS, freqs, 2, BLK, rcvs), jnp.bfloat16),
                pltpu.VMEM((shots, depth), jnp.bfloat16),
                pltpu.VMEM((STEPS, 2, BLK, 2 * rcvs), jnp.bfloat16),
                pltpu.SemaphoreType.DMA((2,)),
                pltpu.SemaphoreType.DMA((2,)),
            ],
        ),
        compiler_params=pltpu.CompilerParams(vmem_limit_bytes=105 * 512 * 1024),
        cost_estimate=pl.CostEstimate(
            flops=2 * freqs * shots * 2 * rcvs * depth,
            bytes_accessed=20 * 1024 * 1024,
            transcendentals=0,
        ),
    )(a_where, b_where, b_row, *a_parts, *b_parts)


def places(block_ids):
    shot, rcv = lax.axis_index("shot"), lax.axis_index("rcv")
    core, z, x_lo = rcv % CORES, rcv // CORES % Z, rcv // (CORES * Z)
    of_core, of_z, of_x = block_ids % CORES, block_ids // CORES % Z, block_ids // (CORES * Z)
    distance = jnp.where(of_core == 0, z - of_z, of_z - z) % Z
    a_where = ((of_core != core) * 2 + (of_x != x_lo)) * Z + distance
    owner = block_ids // 2
    y, of_y = shot % Y, owner % Y
    distance = jnp.where(core == 0, y - of_y, of_y - y) % Y
    b_where = (shot // Y != owner // Y) * Y + distance
    return a_where.astype(jnp.int32), b_where.astype(jnp.int32), block_ids % 2 * BLK


def after(value, *earlier):
    return lax.optimization_barrier((value, *earlier))[0]


def per_device(surface_data, source_traces, block_ids):
    a, b = surface_data, source_traces
    a_where, b_where, b_row = places(block_ids)

    def send(name, value, **way):
        with jax.named_scope(name):
            return moved(value, **way)

    def swap(name, value):
        return send(name, value, flip_core=True)

    b_3 = send("b_3", b, dy=-1)
    b_x = send("b_x", b, dx=2)
    a_3 = send("a_3", a, dz=-1)
    b_1 = send("b_1", b, dy=1)
    a_1 = send("a_1", a, dz=1)
    a_x = send("a_x", after(a, b_3, a_where, b_where, b_row), flip_x=True)
    other_3 = swap("other_3", after(a_3, b_x))
    b_x1 = send("b_x1", after(b_x, a_3), dy=1)
    a_2 = send("a_2", after(a_1, b_1), dz=1)
    b_x3 = send("b_x3", after(b_x, a_1), dy=-1)
    a_x3 = send("a_x3", a_x, dz=-1)
    b_2 = send("b_2", after(b_1, other_3), dy=1)
    a_x2 = send("a_x2", after(a_2, b_x1), flip_x=True)
    b_x2 = send("b_x2", after(b_x1, a_2), dy=1)
    a_x1 = send("a_x1", after(a_x, b_x3), dz=1)
    other = swap("other", after(a, a_x3))
    other_2 = swap("other_2", after(a_2, b_2))
    other_1 = swap("other_1", after(a_1, a_x2))
    other_x2 = swap("other_x2", after(a_x2, b_x2))
    other_x1 = swap("other_x1", a_x1)
    other_x = swap("other_x", after(a_x, other))
    other_x3 = swap("other_x3", after(a_x3, other_2))

    a_parts = [other_x3, other_x, a, a_1, a_2, a_3, a_x, a_x1]
    a_parts += [a_x2, a_x3, other, other_1, other_2, other_3, other_x1, other_x2]
    b_parts = [b, b_1, b_2, b_3, b_x, b_x1, b_x2, b_x3]
    return multiply(a_parts, b_parts, a_where, b_where, b_row)


def solution(mesh):
    in_specs = (P(None, None, "rcv", "shot"), P(None, None, "shot", "rcv"), P())
    out_specs = P(None, None, "shot", "rcv")
    return jax.shard_map(
        per_device, mesh=mesh, in_specs=in_specs, out_specs=out_specs, check_vma=False
    )
```
